32 devices in a mesh: layer: 8 (over z, y), blk: 4 (over x, core).
Axes of the slice: x: 2, y: 2, z: 4, core: 2. Of those that a mesh axis runs over, the one named last changes fastest.
Arguments:
- mode_matrix: bfloat16 [16, 512, 512], P(None, 'layer', 'blk'), may hold values from -1 to 1, as said below
- decay_rate: bfloat16 [16, 512], P(None, 'layer'), may hold values from 0.0009994507 to 0.29882812
- facet_refl: bfloat16 [16, 512], P(None, 'layer'), may hold values from -0.796875 to 0.796875
Outputs:
- prefix: bfloat16 [8, 4, 512, 512], P('layer', None, 'blk')
The draws below stay inside these ranges and needn't reach their ends.
Inputs may be any that keep to these rules, and one draw needn't show every extreme that they name: `mode_matrix`: each layer's matrix has orthonormal columns up to the rounding to bfloat16.
All inputs are finite; a program needn't handle non-finite values.
Results may differ from the reference program's by a relative error of at most 0.0045.
The reference program's roundings to bfloat16 on the way count: a program that leaves them out, or rounds other values in their place, can miss the bound.
Values may be sent and summed in bfloat16 or wider, within the bound.
A program may use at most 64 MiB of HBM per device.

```python
import math
import jax
import jax.numpy as jnp
from jax import lax

HARM = 512
LAY_DEV = 2
REFL = 4
GROUPS = 8
LAYERS = 16
LEVELS = 3


def draw_mode_matrix(key, part):
    layer_keys = jax.random.split(key, LAYERS)

    def make_one(one_key):
        jitter = jax.random.normal(one_key, (HARM, HARM), jnp.float32) * (0.22 / math.sqrt(HARM))
        current = jnp.eye(HARM, dtype=jnp.float32) + jitter
        for repeat in range(8):
            gram = jnp.dot(current.T, current, precision=lax.Precision.HIGHEST)
            current = 1.5 * current - 0.5 * jnp.dot(current, gram, precision=lax.Precision.HIGHEST)
        return current.astype(jnp.bfloat16)
    return lax.map(make_one, layer_keys)


def levels(rng, shape, shards, least, largest):
    gain = 1.0
    for dim, parts in shards:
        steps = jax.random.uniform(jax.random.fold_in(jax.random.fold_in(rng, 6), dim), (parts,), jnp.float32, least / len(shards), largest / len(shards))
        gain = gain * jnp.repeat(jnp.exp(steps), shape[dim] // parts).reshape((-1,) + (1,) * (len(shape) - 1 - dim))
    return gain


def setup_inputs(seed: int = 0) -> dict:
    seeds = jax.random.split(jax.random.key(seed), 4)
    return {
        "mode_matrix": draw_mode_matrix(jax.random.fold_in(seeds[3], 71), 0),
        "decay_rate": jnp.clip(jnp.exp(math.log(0.29882812) - 5.700418 * jax.random.uniform(seeds[1], (LAYERS, HARM), jnp.float32) ** levels(seeds[1], (LAYERS, HARM), ((1, 8),), -0.2, 0.2)), 0.0009994507, 0.29882812).astype(jnp.bfloat16),
        "facet_refl": jnp.clip(jax.random.uniform(seeds[2], (LAYERS, HARM), jnp.float32, -0.796875, 0.796875) * levels(seeds[2], (LAYERS, HARM), ((1, 8),), -0.4, 0.0), -0.796875, 0.796875).astype(jnp.bfloat16),
    }


def times_f32(left_op, right_op):
    return jnp.dot(left_op, right_op, preferred_element_type=jnp.float32)

def star_product(upper_s, lower_s):
    coupling_down = times_f32(lower_s[0], upper_s[3]).astype(jnp.bfloat16)
    coupling_up = times_f32(upper_s[3], lower_s[0]).astype(jnp.bfloat16)
    left_sum = upper_s[1]
    for repeat in range(REFL):
        left_sum = (upper_s[1] + times_f32(left_sum, coupling_down)).astype(jnp.bfloat16)
    right_sum = lower_s[2]
    for repeat in range(REFL):
        right_sum = (lower_s[2] + times_f32(right_sum, coupling_up)).astype(jnp.bfloat16)
    left_mid = times_f32(left_sum, lower_s[0]).astype(jnp.bfloat16)
    right_mid = times_f32(right_sum, upper_s[3]).astype(jnp.bfloat16)
    new_refl = (upper_s[0] + times_f32(left_mid, upper_s[2])).astype(jnp.bfloat16)
    new_back = times_f32(left_sum, lower_s[1]).astype(jnp.bfloat16)
    new_fore = times_f32(right_sum, upper_s[2]).astype(jnp.bfloat16)
    new_under = (lower_s[3] + times_f32(right_mid, lower_s[1])).astype(jnp.bfloat16)
    return jnp.stack([new_refl, new_back, new_fore, new_under])

def layer_blocks(inputs):
    modes_one, decay_one, refl_one = inputs
    refl_full = refl_one.astype(jnp.float32)
    transmit = jnp.sqrt(1.0 - refl_full * refl_full) * jnp.exp(-decay_one.astype(jnp.float32))
    modes_wide = modes_one.astype(jnp.float32)
    scaled_refl = (modes_wide * refl_full[None, :]).astype(jnp.bfloat16)
    scaled_tran = (modes_wide * transmit[None, :]).astype(jnp.bfloat16)
    reflection = times_f32(modes_one, scaled_refl.T).astype(jnp.bfloat16)
    transmission = times_f32(modes_one, scaled_tran.T).astype(jnp.bfloat16)
    return jnp.stack([reflection, transmission, transmission, -reflection])

def group_fold(stack_group):
    running = stack_group[0]
    for layer_pos in range(1, LAY_DEV):
        running = star_product(running, stack_group[layer_pos])
    return running

def pair_star(operands):
    return star_product(operands[0], operands[1])

def reference(mode_matrix, decay_rate, facet_refl):
    layer_s = lax.map(layer_blocks, (mode_matrix, decay_rate, facet_refl))
    grouped = layer_s.reshape(GROUPS, LAY_DEV, 4, HARM, HARM)
    prefix = lax.map(group_fold, grouped)
    group_ids = jnp.arange(GROUPS, dtype=jnp.int32)
    for section_level in range(LEVELS):
        distance = 2 ** section_level
        shifted = jnp.concatenate([jnp.zeros_like(prefix[:distance]), prefix[:-distance]], axis=0)
        combined = lax.map(pair_star, (shifted, prefix))
        keep_new = (group_ids >= distance)[:, None, None, None]
        prefix = jnp.where(keep_new, combined, prefix)
    return prefix
```

```python
import functools

import jax
import jax.numpy as jnp
from jax import lax
from jax.experimental import pallas as pl
from jax.experimental.pallas import tpu as pltpu
from jax.sharding import PartitionSpec as P

REFL = 4
LANES = 128
MESH = pl.DeviceIdType.MESH


def dot(left_op, right_op):
    return jnp.dot(left_op, right_op, preferred_element_type=jnp.float32)


def stack_kernel(
    n, nb, levels,
    mode_ref, aux_ref, out_ref,
    mrecv, arecv, modes, scaled, layer_s, state, land,
    down, up, left, right, mid,
    mode_send, mode_recv, aux_send, aux_recv, share_send, share_recv,
    far_send, far_recv, relay_send, relay_recv,
):
    group = lax.axis_index("layer")
    blk = lax.axis_index("blk")
    cross = lax.rem(blk + 2, nb)
    sib = blk + 1 - 2 * lax.rem(blk, 2)
    sib_cross = lax.rem(sib + 2, nb)
    harm = state.shape[-1]
    rows = harm // nb
    lay = mode_ref.shape[0] // n
    mode_local = harm // n

    def block_rows(index):
        return pl.ds(pl.multiple_of(index * rows, rows), rows)

    own = block_rows(blk)

    barrier = pltpu.get_barrier_semaphore()

    def greet(offset, carry):
        pl.semaphore_signal(
            barrier, inc=1, device_id=(lax.rem(group + offset, n), blk), device_id_type=MESH
        )
        return carry

    lax.fori_loop(1, n, greet, 0)
    for other in (cross, sib):
        pl.semaphore_signal(barrier, inc=1, device_id=(group, other), device_id_type=MESH)
    pl.semaphore_wait(barrier, n + 1)

    def mode_copy(offset):
        target = lax.rem(group + offset, n)
        return pltpu.make_async_remote_copy(
            src_ref=mode_ref.at[pl.ds(target * lay, lay)],
            dst_ref=mrecv.at[blk, group],
            send_sem=mode_send.at[offset],
            recv_sem=mode_recv.at[offset],
            device_id=(target, blk),
            device_id_type=MESH,
        )

    def aux_copy(offset):
        target = lax.rem(group + offset, n)
        return pltpu.make_async_remote_copy(
            src_ref=aux_ref.at[target],
            dst_ref=arecv.at[group],
            send_sem=aux_send.at[offset],
            recv_sem=aux_recv.at[offset],
            device_id=(target, blk),
            device_id_type=MESH,
        )

    def start_modes(offset, carry):
        mode_copy(offset).start()
        aux_copy(offset).start()
        return carry

    lax.fori_loop(1, n, start_modes, 0)
    mrecv[blk, group] = mode_ref[pl.ds(group * lay, lay)]
    arecv[group] = aux_ref[group]

    def end_modes(offset, carry):
        mode_copy(offset).wait_recv()
        aux_copy(offset).wait_recv()
        return carry

    lax.fori_loop(1, n, end_modes, 0)

    def share_copy(index, piece, other):
        return pltpu.make_async_remote_copy(
            src_ref=mrecv.at[piece],
            dst_ref=mrecv.at[piece],
            send_sem=share_send.at[index],
            recv_sem=share_recv.at[index],
            device_id=(group, other),
            device_id_type=MESH,
        )

    share_copy(0, blk, cross).start()
    share_copy(1, blk, sib).start()
    share_copy(0, cross, cross).wait_recv()
    share_copy(2, cross, sib).start()
    share_copy(1, sib, sib).wait_recv()
    share_copy(2, sib_cross, sib).wait_recv()

    per_window = LANES // mode_local
    windows = [
        sum(arecv[index] for index in range(w * per_window, (w + 1) * per_window))
        for w in range(harm // LANES)
    ]
    for layer in range(lay):
        for piece in range(nb):
            cols = slice(piece * rows, (piece + 1) * rows)
            wide = mrecv[piece, :, layer].astype(jnp.float32).reshape(harm, rows)
            modes[:, cols] = wide.astype(jnp.bfloat16)
            coeff = windows[piece]
            scaled[0, :, cols] = (wide * coeff[lay + layer][None]).astype(jnp.bfloat16)
            scaled[1, :, cols] = (wide * coeff[layer][None]).astype(jnp.bfloat16)
        for kind in range(2):
            layer_s[layer, kind] = lax.dot_general(
                modes[...], scaled[kind], (((1,), (1,)), ((), ())),
                preferred_element_type=jnp.float32,
            ).astype(jnp.bfloat16)
        layer_s[layer, 2] = -layer_s[layer, 0]

    def far_copy(level, distance, slot, part):
        return pltpu.make_async_remote_copy(
            src_ref=state.at[slot, part, own],
            dst_ref=land.at[level, part, own],
            send_sem=far_send.at[level, part],
            recv_sem=far_recv.at[level, part],
            device_id=(lax.rem(group + distance, n), blk),
            device_id_type=MESH,
        )

    def send_far(level, distance, slot, part):
        @pl.when(group + distance < n)
        def _():
            far_copy(level, distance, slot, part).start()

    def relay_copy(level, part, index, piece, other):
        where = land.at[level, part, block_rows(piece)]
        return pltpu.make_async_remote_copy(
            src_ref=where,
            dst_ref=where,
            send_sem=relay_send.at[level, part, index],
            recv_sem=relay_recv.at[level, part, index],
            device_id=(group, other),
            device_id_type=MESH,
        )

    def relay_first(level, part):
        far_copy(level, 1, 0, part).wait_recv()
        relay_copy(level, part, 0, blk, cross).start()
        relay_copy(level, part, 1, blk, sib).start()

    def relay_second(level, part):
        relay_copy(level, part, 0, cross, cross).wait_recv()
        relay_copy(level, part, 2, cross, sib).start()

    def relay_end(level, part):
        relay_copy(level, part, 1, sib, sib).wait_recv()
        relay_copy(level, part, 2, sib_cross, sib).wait_recv()

    def chain(total, start, coupling, repeats, first):
        for repeat in range(repeats):
            source = start if first and repeat == 0 else total
            total[...] = (start[...] + dot(source[...], coupling[...])).astype(jnp.bfloat16)

    def full_star(a11, a12, a21, a22, b11, b12, b21, b22, into, send, hooks):
        hooks[0]()
        up[...] = dot(a22[...], b11[...]).astype(jnp.bfloat16)
        chain(right, b21, up, 2, True)
        hooks[1]()
        chain(right, b21, up, 2, False)
        mid[...] = dot(right[...], a22[...]).astype(jnp.bfloat16)
        into[3] = (b22[...] + dot(mid[...], b12[...])).astype(jnp.bfloat16)
        send(3)
        down[...] = dot(b11[...], a22[...]).astype(jnp.bfloat16)
        hooks[2]()
        chain(left, a12, down, REFL, True)
        into[1] = dot(left[...], b12[...]).astype(jnp.bfloat16)
        send(1)
        hooks[3]()
        into[2] = dot(right[...], a21[...]).astype(jnp.bfloat16)
        send(2)
        mid[...] = dot(left[...], b11[...]).astype(jnp.bfloat16)
        hooks[4]()
        into[0] = (a11[...] + dot(mid[...], a21[...])).astype(jnp.bfloat16)
        send(0)

    def parts(ref):
        return [ref.at[part] for part in range(4)]

    def layer_parts(layer):
        refl, tran, back = [layer_s.at[layer, kind] for kind in range(3)]
        return [refl, tran, tran, back]

    nothing = [lambda: None] * 5
    last = levels - 1
    assert lay == 2
    full_star(
        *layer_parts(0), *layer_parts(1), state.at[0],
        lambda part: send_far(0, 1, 0, part), nothing,
    )

    slot_end = sum(jnp.where(group >= (1 << k), 1, 0) for k in range(last))

    def one_level(level, distance):
        @pl.when(group >= distance)
        def _():
            def hook0():
                relay_first(level, 3)
                relay_first(level, 1)
                relay_second(level, 3)
                relay_end(level, 3)

            def hook1():
                relay_first(level, 2)
                relay_second(level, 1)

            def hook2():
                relay_end(level, 1)
                relay_first(level, 0)
                relay_second(level, 2)

            def hook3():
                relay_end(level, 2)
                relay_second(level, 0)

            def hook4():
                relay_end(level, 0)

            full_star(
                *parts(land.at[level]), *parts(state.at[level]), state.at[level + 1],
                lambda part: send_far(level + 1, 2 * distance, level + 1, part),
                [hook0, hook1, hook2, hook3, hook4],
            )

        @pl.when(group < distance)
        def _():
            for part in (3, 1, 2, 0):
                send_far(level + 1, 2 * distance, slot_end, part)

        return 2 * distance

    lax.fori_loop(0, last, one_level, 1)

    half = 1 << last

    @pl.when(group < half)
    def _():
        out_ref[...] = state[slot_end, :, own]

    @pl.when(group >= half)
    def _():
        a11, a12, a21, a22 = parts(land.at[last])
        b11, b12, b21, b22 = parts(state.at[last])
        right_rows, left_rows = right.at[:rows], left.at[:rows]
        relay_first(last, 3)
        relay_second(last, 3)
        relay_end(last, 3)
        up[...] = dot(a22[...], b11[...]).astype(jnp.bfloat16)
        down[...] = dot(b11[...], a22[...]).astype(jnp.bfloat16)
        far_copy(last, 1, 0, 1).wait_recv()
        relay_first(last, 2)
        chain(right_rows, b21.at[own], up, REFL, True)
        chain(left_rows, a12.at[own], down, REFL, True)
        right_mid = dot(right_rows[...], a22[...]).astype(jnp.bfloat16)
        left_mid = dot(left_rows[...], b11[...]).astype(jnp.bfloat16)
        out_ref[1] = dot(left_rows[...], b12[...]).astype(jnp.bfloat16)
        out_ref[3] = (b22[own] + dot(right_mid, b12[...])).astype(jnp.bfloat16)
        relay_second(last, 2)
        relay_end(last, 2)
        out_ref[2] = dot(right_rows[...], a21[...]).astype(jnp.bfloat16)
        far_copy(last, 1, 0, 0).wait_recv()
        out_ref[0] = (a11[own] + dot(left_mid, a21[...])).astype(jnp.bfloat16)

    def leave_modes(offset, carry):
        mode_copy(offset).wait_send()
        aux_copy(offset).wait_send()
        return carry

    lax.fori_loop(1, n, leave_modes, 0)
    share_copy(0, blk, cross).wait_send()
    share_copy(1, blk, sib).wait_send()
    share_copy(2, cross, sib).wait_send()
    for level in range(levels):
        @pl.when(group + (1 << level) < n)
        def _(level=level):
            for part in range(4):
                far_copy(level, 1, 0, part).wait_send()

        @pl.when(group >= (1 << level))
        def _(level=level):
            for part in range(4) if level < last else (2, 3):
                relay_copy(level, part, 0, blk, cross).wait_send()
                relay_copy(level, part, 1, blk, sib).wait_send()
                relay_copy(level, part, 2, cross, sib).wait_send()


def on_device(n, nb, mode_matrix, decay_rate, facet_refl):
    layers, mode_local = decay_rate.shape
    harm = n * mode_matrix.shape[1]
    lay = layers // n
    levels = n.bit_length() - 1
    refl = facet_refl.astype(jnp.float32)
    tran = jnp.sqrt(1.0 - refl * refl) * jnp.exp(-decay_rate.astype(jnp.float32))
    coeff = jnp.concatenate(
        [tran.reshape(n, lay, mode_local), refl.reshape(n, lay, mode_local)], axis=1
    )
    coeff = jnp.pad(coeff, ((0, 0), (0, 8 - 2 * lay), (0, 0)))
    copies = LANES // mode_local
    place = lax.broadcasted_iota(jnp.int32, (1, 1, LANES), 2) // mode_local
    aux = jnp.where(
        place == lax.rem(lax.axis_index("layer"), copies), jnp.tile(coeff, (1, 1, copies)), 0.0
    )
    square = (harm, harm)
    dma = pltpu.SemaphoreType.DMA
    vmem = pl.BlockSpec(memory_space=pltpu.VMEM)
    result = pl.pallas_call(
        functools.partial(stack_kernel, n, nb, levels),
        out_shape=jax.ShapeDtypeStruct((4, harm // nb, harm), jnp.bfloat16),
        in_specs=[vmem, vmem],
        out_specs=vmem,
        scratch_shapes=[
            pltpu.VMEM((nb, n, lay) + mode_matrix.shape[1:], jnp.bfloat16),
            pltpu.VMEM((n, 8, LANES), jnp.float32),
            pltpu.VMEM(square, jnp.bfloat16),
            pltpu.VMEM((2,) + square, jnp.bfloat16),
            pltpu.VMEM((lay, 3) + square, jnp.bfloat16),
            pltpu.VMEM((levels, 4) + square, jnp.bfloat16),
            pltpu.VMEM((levels, 4) + square, jnp.bfloat16),
        ]
        + [pltpu.VMEM(square, jnp.bfloat16)] * 5
        + [dma((n,))] * 4
        + [dma((3,))] * 2
        + [dma((levels, 4))] * 2
        + [dma((levels, 4, 3))] * 2,
        compiler_params=pltpu.CompilerParams(
            collective_id=0, has_side_effects=True, vmem_limit_bytes=56 * 1024 * 1024
        ),
        cost_estimate=pl.CostEstimate(
            flops=2 * harm**3 * 60, bytes_accessed=2**20, transcendentals=0
        ),
    )(mode_matrix, aux)
    return result[None]


def solution(mesh):
    n, nb = mesh.shape["layer"], mesh.shape["blk"]
    placed = (P(None, "layer", "blk"), P(None, "layer"), P(None, "layer"))
    return jax.shard_map(
        functools.partial(on_device, n, nb),
        mesh=mesh,
        in_specs=placed,
        out_specs=P("layer", None, "blk", None),
        check_vma=False,
    )
```

```python
import functools

import jax
import jax.numpy as jnp
from jax import lax
from jax.experimental import pallas as pl
from jax.experimental.pallas import tpu as pltpu
from jax.sharding import PartitionSpec as P

REFL = 4
LANES = 128
HALVES = 2
MESH = pl.DeviceIdType.MESH


def dot(left_op, right_op):
    return jnp.dot(left_op, right_op, preferred_element_type=jnp.float32)


def stack_kernel(
    n, nb, levels,
    mode_ref, aux_ref, out_ref,
    mrecv, arecv, modes, scaled, layer_s, state, land,
    down, up, left, right, mid,
    mode_send, mode_recv, aux_send, aux_recv, share_send, share_recv,
    far_send, far_recv, relay_send, relay_recv,
):
    group = lax.axis_index("layer")
    blk = lax.axis_index("blk")
    cross = lax.rem(blk + 2, nb)
    sib = blk + 1 - 2 * lax.rem(blk, 2)
    sib_cross = lax.rem(sib + 2, nb)
    harm = state.shape[-1]
    rows = harm // nb
    lay = mode_ref.shape[0] // n
    mode_local = harm // n

    def block_rows(index):
        return pl.ds(pl.multiple_of(index * rows, rows), rows)

    own = block_rows(blk)

    barrier = pltpu.get_barrier_semaphore()

    def greet(offset, carry):
        pl.semaphore_signal(
            barrier, inc=1, device_id=(lax.rem(group + offset, n), blk), device_id_type=MESH
        )
        return carry

    lax.fori_loop(1, n, greet, 0)
    for other in (cross, sib):
        pl.semaphore_signal(barrier, inc=1, device_id=(group, other), device_id_type=MESH)
    pl.semaphore_wait(barrier, n + 1)

    def mode_copy(offset, layer):
        target = lax.rem(group + offset, n)
        return pltpu.make_async_remote_copy(
            src_ref=mode_ref.at[target * lay + layer],
            dst_ref=mrecv.at[blk, layer, group],
            send_sem=mode_send.at[offset, layer],
            recv_sem=mode_recv.at[offset, layer],
            device_id=(target, blk),
            device_id_type=MESH,
        )

    def aux_copy(offset):
        target = lax.rem(group + offset, n)
        return pltpu.make_async_remote_copy(
            src_ref=aux_ref.at[target],
            dst_ref=arecv.at[group],
            send_sem=aux_send.at[offset],
            recv_sem=aux_recv.at[offset],
            device_id=(target, blk),
            device_id_type=MESH,
        )

    def for_offsets(body):
        def step(offset, carry):
            body(offset)
            return carry

        lax.fori_loop(1, n, step, 0)

    for layer in range(lay):
        for_offsets(lambda offset: mode_copy(offset, layer).start())
        if layer == 0:
            for_offsets(lambda offset: aux_copy(offset).start())
        mrecv[blk, layer, group] = mode_ref[group * lay + layer]
    arecv[group] = aux_ref[group]

    def share_copy(layer, index, piece, other):
        return pltpu.make_async_remote_copy(
            src_ref=mrecv.at[piece, layer],
            dst_ref=mrecv.at[piece, layer],
            send_sem=share_send.at[layer, index],
            recv_sem=share_recv.at[layer, index],
            device_id=(group, other),
            device_id_type=MESH,
        )

    for layer in range(lay):
        for_offsets(lambda offset: mode_copy(offset, layer).wait_recv())
        share_copy(layer, 0, blk, cross).start()
        share_copy(layer, 1, blk, sib).start()
    for_offsets(lambda offset: aux_copy(offset).wait_recv())
    per_window = LANES // mode_local
    windows = [
        sum(arecv[index] for index in range(w * per_window, (w + 1) * per_window))
        for w in range(harm // LANES)
    ]

    for layer in range(lay):
        share_copy(layer, 0, cross, cross).wait_recv()
        share_copy(layer, 2, cross, sib).start()
        share_copy(layer, 1, sib, sib).wait_recv()
        share_copy(layer, 2, sib_cross, sib).wait_recv()
        for piece in range(nb):
            cols = slice(piece * rows, (piece + 1) * rows)
            wide = mrecv[piece, layer].astype(jnp.float32).reshape(harm, rows)
            modes[:, cols] = wide.astype(jnp.bfloat16)
            coeff = windows[piece]
            scaled[0, :, cols] = (wide * coeff[lay + layer][None]).astype(jnp.bfloat16)
            scaled[1, :, cols] = (wide * coeff[layer][None]).astype(jnp.bfloat16)
        for kind in range(2):
            layer_s[layer, kind] = lax.dot_general(
                modes[...], scaled[kind], (((1,), (1,)), ((), ())),
                preferred_element_type=jnp.float32,
            ).astype(jnp.bfloat16)
        layer_s[layer, 2] = -layer_s[layer, 0]

    def piece_rows(index, half):
        size = rows // HALVES
        return pl.ds(pl.multiple_of(index * rows + half * size, size), size)

    def far_copy(level, distance, slot, part, half):
        return pltpu.make_async_remote_copy(
            src_ref=state.at[slot, part, piece_rows(blk, half)],
            dst_ref=land.at[level, part, piece_rows(blk, half)],
            send_sem=far_send.at[level, part, half],
            recv_sem=far_recv.at[level, part, half],
            device_id=(lax.rem(group + distance, n), blk),
            device_id_type=MESH,
        )

    def send_far(level, distance, slot, part):
        @pl.when(group + distance < n)
        def _():
            for half in range(HALVES):
                far_copy(level, distance, slot, part, half).start()

    def far_left(level):
        for part in range(4):
            for half in range(HALVES):
                far_copy(level, 1, 0, part, half).wait_send()

    def relay_copy(level, part, half, index, piece, other):
        where = land.at[level, part, piece_rows(piece, half)]
        return pltpu.make_async_remote_copy(
            src_ref=where,
            dst_ref=where,
            send_sem=relay_send.at[level, part, half, index],
            recv_sem=relay_recv.at[level, part, half, index],
            device_id=(group, other),
            device_id_type=MESH,
        )

    def relay_first(level, part, half):
        far_copy(level, 1, 0, part, half).wait_recv()
        relay_copy(level, part, half, 0, blk, cross).start()
        relay_copy(level, part, half, 1, blk, sib).start()

    def relay_second(level, part, half):
        relay_copy(level, part, half, 0, cross, cross).wait_recv()
        relay_copy(level, part, half, 2, cross, sib).start()

    def relay_end(level, part):
        for half in range(HALVES):
            relay_copy(level, part, half, 1, sib, sib).wait_recv()
            relay_copy(level, part, half, 2, sib_cross, sib).wait_recv()

    def chain(total, start, coupling, repeat):
        source = start if repeat == 0 else total
        total[...] = (start[...] + dot(source[...], coupling[...])).astype(jnp.bfloat16)

    def full_star(a11, a12, a21, a22, b11, b12, b21, b22, into, send, first, second, end):
        first(3, 0)
        first(3, 1)
        second(3, 0)
        first(1, 0)
        second(3, 1)
        end(3)
        up[...] = dot(a22[...], b11[...]).astype(jnp.bfloat16)
        first(1, 1)
        chain(right, b21, up, 0)
        second(1, 0)
        chain(right, b21, up, 1)
        chain(right, b21, up, 2)
        second(1, 1)
        chain(right, b21, up, 3)
        mid[...] = dot(right[...], a22[...]).astype(jnp.bfloat16)
        into[3] = (b22[...] + dot(mid[...], b12[...])).astype(jnp.bfloat16)
        send(3)
        first(2, 0)
        down[...] = dot(b11[...], a22[...]).astype(jnp.bfloat16)
        first(2, 1)
        end(1)
        chain(left, a12, down, 0)
        second(2, 0)
        first(0, 0)
        chain(left, a12, down, 1)
        second(2, 1)
        first(0, 1)
        chain(left, a12, down, 2)
        second(0, 0)
        chain(left, a12, down, 3)
        into[1] = dot(left[...], b12[...]).astype(jnp.bfloat16)
        send(1)
        second(0, 1)
        end(2)
        into[2] = dot(right[...], a21[...]).astype(jnp.bfloat16)
        send(2)
        mid[...] = dot(left[...], b11[...]).astype(jnp.bfloat16)
        end(0)
        into[0] = (a11[...] + dot(mid[...], a21[...])).astype(jnp.bfloat16)
        send(0)

    def parts(ref):
        return [ref.at[part] for part in range(4)]

    def layer_parts(layer):
        refl, tran, back = [layer_s.at[layer, kind] for kind in range(3)]
        return [refl, tran, tran, back]

    def nothing(*where):
        pass

    last = levels - 1
    assert lay == 2
    full_star(
        *layer_parts(0), *layer_parts(1), state.at[0],
        lambda part: send_far(0, 1, 0, part), nothing, nothing, nothing,
    )

    slot_end = sum(jnp.where(group >= (1 << k), 1, 0) for k in range(last))

    def one_level(level, distance):
        @pl.when(group >= distance)
        def _():
            full_star(
                *parts(land.at[level]), *parts(state.at[level]), state.at[level + 1],
                lambda part: send_far(level + 1, 2 * distance, level + 1, part),
                functools.partial(relay_first, level),
                functools.partial(relay_second, level),
                functools.partial(relay_end, level),
            )

        @pl.when(group < distance)
        def _():
            far_left(level)
            for part in (3, 1, 2, 0):
                send_far(level + 1, 2 * distance, slot_end, part)

        return 2 * distance

    lax.fori_loop(0, last, one_level, 1)

    half = 1 << last

    @pl.when(group < half)
    def _():
        out_ref[...] = state[slot_end, :, own]

    @pl.when(group >= half)
    def _():
        a11, a12, a21, a22 = parts(land.at[last])
        b11, b12, b21, b22 = parts(state.at[last])
        right_rows, left_rows = right.at[:rows], left.at[:rows]
        relay_first(last, 3, 0)
        relay_first(last, 3, 1)
        relay_second(last, 3, 0)
        relay_second(last, 3, 1)
        relay_end(last, 3)
        up[...] = dot(a22[...], b11[...]).astype(jnp.bfloat16)
        down[...] = dot(b11[...], a22[...]).astype(jnp.bfloat16)
        for half in range(HALVES):
            far_copy(last, 1, 0, 1, half).wait_recv()
        for repeat in range(REFL):
            chain(right_rows, b21.at[own], up, repeat)
            chain(left_rows, a12.at[own], down, repeat)
        relay_first(last, 2, 0)
        right_mid = dot(right_rows[...], a22[...]).astype(jnp.bfloat16)
        left_mid = dot(left_rows[...], b11[...]).astype(jnp.bfloat16)
        relay_first(last, 2, 1)
        out_ref[1] = dot(left_rows[...], b12[...]).astype(jnp.bfloat16)
        relay_second(last, 2, 0)
        out_ref[3] = (b22[own] + dot(right_mid, b12[...])).astype(jnp.bfloat16)
        relay_second(last, 2, 1)
        relay_end(last, 2)
        out_ref[2] = dot(right_rows[...], a21[...]).astype(jnp.bfloat16)
        for half in range(HALVES):
            far_copy(last, 1, 0, 0, half).wait_recv()
        out_ref[0] = (a11[own] + dot(left_mid, a21[...])).astype(jnp.bfloat16)

    for layer in range(lay):
        for_offsets(lambda offset: mode_copy(offset, layer).wait_send())
        share_copy(layer, 0, blk, cross).wait_send()
        share_copy(layer, 1, blk, sib).wait_send()
        share_copy(layer, 2, cross, sib).wait_send()
    for_offsets(lambda offset: aux_copy(offset).wait_send())
    for level in range(levels):
        reach = 1 << level
        sends = group + reach < n
        if level < last:
            sends = jnp.logical_and(sends, group >= reach)

        @pl.when(sends)
        def _(level=level):
            far_left(level)

        @pl.when(group >= reach)
        def _(level=level):
            for part in range(4) if level < last else (2, 3):
                for half in range(HALVES):
                    relay_copy(level, part, half, 0, blk, cross).wait_send()
                    relay_copy(level, part, half, 1, blk, sib).wait_send()
                    relay_copy(level, part, half, 2, cross, sib).wait_send()


def on_device(n, nb, mode_matrix, decay_rate, facet_refl):
    layers, mode_local = decay_rate.shape
    harm = n * mode_matrix.shape[1]
    lay = layers // n
    levels = n.bit_length() - 1
    refl = facet_refl.astype(jnp.float32)
    tran = jnp.sqrt(1.0 - refl * refl) * jnp.exp(-decay_rate.astype(jnp.float32))
    coeff = jnp.concatenate(
        [tran.reshape(n, lay, mode_local), refl.reshape(n, lay, mode_local)], axis=1
    )
    coeff = jnp.pad(coeff, ((0, 0), (0, 8 - 2 * lay), (0, 0)))
    copies = LANES // mode_local
    place = lax.broadcasted_iota(jnp.int32, (1, 1, LANES), 2) // mode_local
    aux = jnp.where(
        place == lax.rem(lax.axis_index("layer"), copies), jnp.tile(coeff, (1, 1, copies)), 0.0
    )
    square = (harm, harm)
    dma = pltpu.SemaphoreType.DMA
    vmem = pl.BlockSpec(memory_space=pltpu.VMEM)
    result = pl.pallas_call(
        functools.partial(stack_kernel, n, nb, levels),
        out_shape=jax.ShapeDtypeStruct((4, harm // nb, harm), jnp.bfloat16),
        in_specs=[vmem, vmem],
        out_specs=vmem,
        scratch_shapes=[
            pltpu.VMEM((nb, lay, n) + mode_matrix.shape[1:], jnp.bfloat16),
            pltpu.VMEM((n, 8, LANES), jnp.float32),
            pltpu.VMEM(square, jnp.bfloat16),
            pltpu.VMEM((2,) + square, jnp.bfloat16),
            pltpu.VMEM((lay, 3) + square, jnp.bfloat16),
            pltpu.VMEM((levels, 4) + square, jnp.bfloat16),
            pltpu.VMEM((levels, 4) + square, jnp.bfloat16),
        ]
        + [pltpu.VMEM(square, jnp.bfloat16)] * 5
        + [dma((n, lay))] * 2
        + [dma((n,))] * 2
        + [dma((lay, 3))] * 2
        + [dma((levels, 4, HALVES))] * 2
        + [dma((levels, 4, HALVES, 3))] * 2,
        compiler_params=pltpu.CompilerParams(
            collective_id=0, has_side_effects=True, vmem_limit_bytes=56 * 1024 * 1024
        ),
        cost_estimate=pl.CostEstimate(
            flops=2 * harm**3 * 60, bytes_accessed=2**20, transcendentals=0
        ),
    )(mode_matrix, aux)
    return result[None]


def solution(mesh):
    n, nb = mesh.shape["layer"], mesh.shape["blk"]
    placed = (P(None, "layer", "blk"), P(None, "layer"), P(None, "layer"))
    return jax.shard_map(
        functools.partial(on_device, n, nb),
        mesh=mesh,
        in_specs=placed,
        out_specs=P("layer", None, "blk", None),
        check_vma=False,
    )
```

```python
import functools

import jax
import jax.numpy as jnp
from jax import lax
from jax.experimental import pallas as pl
from jax.experimental.pallas import tpu as pltpu
from jax.sharding import PartitionSpec as P

REFL = 4
LANES = 128
HALVES = 2
MESH = pl.DeviceIdType.MESH


def dot(left_op, right_op):
    return jnp.dot(left_op, right_op, preferred_element_type=jnp.float32)


def stack_kernel(
    n, nb, levels,
    mode_ref, aux_ref, out_ref,
    mrecv, arecv, modes, scaled, layer_s, state, land,
    down, up, left, right, mid,
    mode_send, mode_recv, aux_send, aux_recv, share_send, share_recv,
    far_send, far_recv, relay_send, relay_recv, pair_send, pair_recv,
):
    group = lax.axis_index("layer")
    blk = lax.axis_index("blk")
    cross = lax.rem(blk + 2, nb)
    sib = blk + 1 - 2 * lax.rem(blk, 2)
    sib_cross = lax.rem(sib + 2, nb)
    harm = state.shape[-1]
    rows = harm // nb
    lay = mode_ref.shape[0] // n
    mode_local = harm // n

    def place(quarter):
        return lax.rem(quarter, 2) * (nb // 2) + lax.div(quarter, 2)

    def fixed_place(quarter):
        return quarter % 2 * (nb // 2) + quarter // 2

    def cut(index):
        return slice(index * rows, (index + 1) * rows)

    own = pl.ds(pl.multiple_of(place(blk) * rows, rows), rows)
    wing = harm // 2
    half_rows = pl.ds(pl.multiple_of(lax.rem(blk, 2) * wing, wing), wing)

    barrier = pltpu.get_barrier_semaphore()

    def greet(offset, carry):
        pl.semaphore_signal(
            barrier, inc=1, device_id=(lax.rem(group + offset, n), blk), device_id_type=MESH
        )
        return carry

    lax.fori_loop(1, n, greet, 0)
    for other in (cross, sib):
        pl.semaphore_signal(barrier, inc=1, device_id=(group, other), device_id_type=MESH)
    pl.semaphore_wait(barrier, n + 1)

    def mode_copy(offset, layer):
        target = lax.rem(group + offset, n)
        return pltpu.make_async_remote_copy(
            src_ref=mode_ref.at[target * lay + layer],
            dst_ref=mrecv.at[blk, layer, group],
            send_sem=mode_send.at[offset, layer],
            recv_sem=mode_recv.at[offset, layer],
            device_id=(target, blk),
            device_id_type=MESH,
        )

    def aux_copy(offset):
        target = lax.rem(group + offset, n)
        return pltpu.make_async_remote_copy(
            src_ref=aux_ref.at[target],
            dst_ref=arecv.at[group],
            send_sem=aux_send.at[offset],
            recv_sem=aux_recv.at[offset],
            device_id=(target, blk),
            device_id_type=MESH,
        )

    def for_offsets(body):
        def step(offset, carry):
            body(offset)
            return carry

        lax.fori_loop(1, n, step, 0)

    for layer in range(lay):
        for_offsets(lambda offset: mode_copy(offset, layer).start())
        if layer == 0:
            for_offsets(lambda offset: aux_copy(offset).start())
        mrecv[blk, layer, group] = mode_ref[group * lay + layer]
    arecv[group] = aux_ref[group]

    def share_copy(layer, index, piece, other):
        return pltpu.make_async_remote_copy(
            src_ref=mrecv.at[piece, layer],
            dst_ref=mrecv.at[piece, layer],
            send_sem=share_send.at[layer, index],
            recv_sem=share_recv.at[layer, index],
            device_id=(group, other),
            device_id_type=MESH,
        )

    for layer in range(lay):
        for_offsets(lambda offset: mode_copy(offset, layer).wait_recv())
        share_copy(layer, 0, blk, cross).start()
        share_copy(layer, 1, blk, sib).start()
    for_offsets(lambda offset: aux_copy(offset).wait_recv())
    per_window = LANES // mode_local
    windows = [
        sum(arecv[index] for index in range(w * per_window, (w + 1) * per_window))
        for w in range(harm // LANES)
    ]

    for layer in range(lay):
        share_copy(layer, 0, cross, cross).wait_recv()
        share_copy(layer, 2, cross, sib).start()
        share_copy(layer, 1, sib, sib).wait_recv()
        share_copy(layer, 2, sib_cross, sib).wait_recv()
        for piece in range(nb):
            cols = cut(piece)
            wide = mrecv[piece, layer].astype(jnp.float32).reshape(harm, rows)
            coeff = windows[piece]
            for quarter in range(nb):
                some, where = wide[cut(quarter)], cut(fixed_place(quarter))
                modes[where, cols] = some.astype(jnp.bfloat16)
                scaled[0, where, cols] = (some * coeff[lay + layer][None]).astype(jnp.bfloat16)
                scaled[1, where, cols] = (some * coeff[layer][None]).astype(jnp.bfloat16)
        for kind in range(2):
            layer_s[layer, kind] = lax.dot_general(
                modes[...], scaled[kind], (((1,), (1,)), ((), ())),
                preferred_element_type=jnp.float32,
            ).astype(jnp.bfloat16)
        layer_s[layer, 2] = -layer_s[layer, 0]

    def piece_rows(quarter, half):
        size = rows // HALVES
        return pl.ds(pl.multiple_of(place(quarter) * rows + half * size, size), size)

    def far_copy(level, distance, slot, part, half):
        return pltpu.make_async_remote_copy(
            src_ref=state.at[slot, part, piece_rows(blk, half)],
            dst_ref=land.at[level, part, piece_rows(blk, half)],
            send_sem=far_send.at[level, part, half],
            recv_sem=far_recv.at[level, part, half],
            device_id=(lax.rem(group + distance, n), blk),
            device_id_type=MESH,
        )

    def send_far(level, distance, slot, part):
        @pl.when(group + distance < n)
        def _():
            for half in range(HALVES):
                far_copy(level, distance, slot, part, half).start()

    def far_left(level):
        for part in range(4):
            for half in range(HALVES):
                far_copy(level, 1, 0, part, half).wait_send()

    def pair_copy(slot, part, where):
        return pltpu.make_async_remote_copy(
            src_ref=state.at[slot, part, where],
            dst_ref=state.at[slot, part, where],
            send_sem=pair_send.at[slot, part],
            recv_sem=pair_recv.at[slot, part],
            device_id=(group, sib),
            device_id_type=MESH,
        )

    def settle(slot):
        for part in range(2):
            pair_copy(slot, part, half_rows).wait_recv()

    def relay_copy(level, part, half, index, piece, other):
        where = land.at[level, part, piece_rows(piece, half)]
        return pltpu.make_async_remote_copy(
            src_ref=where,
            dst_ref=where,
            send_sem=relay_send.at[level, part, half, index],
            recv_sem=relay_recv.at[level, part, half, index],
            device_id=(group, other),
            device_id_type=MESH,
        )

    def relay_first(level, part):
        for half in range(HALVES):
            far_copy(level, 1, 0, part, half).wait_recv()
            relay_copy(level, part, half, 0, blk, cross).start()
            if part >= 2:
                relay_copy(level, part, half, 1, blk, sib).start()

    def relay_second(level, part):
        for half in range(HALVES):
            relay_copy(level, part, half, 0, cross, cross).wait_recv()
            if part >= 2:
                relay_copy(level, part, half, 2, cross, sib).start()

    def relay_end(level, part):
        for half in range(HALVES):
            relay_copy(level, part, half, 1, sib, sib).wait_recv()
            relay_copy(level, part, half, 2, sib_cross, sib).wait_recv()

    def chain(total, start, coupling, repeat):
        source = start if repeat == 0 else total
        total[...] = (start[...] + dot(source[...], coupling[...])).astype(jnp.bfloat16)

    def full_star(upper, lower, slot, send, first, second, end, ready):
        a11, a12, a21, a22 = upper
        b11, b12, b21, b22 = lower
        a11, a12, b21, b22 = [ref.at[half_rows] for ref in (a11, a12, b21, b22)]
        into = [state.at[slot, part, half_rows] for part in range(4)]
        first(3)
        second(3)
        ready()
        end(3)
        up[...] = dot(a22[...], b11[...]).astype(jnp.bfloat16)
        first(2)
        chain(right, b21, up, 0)
        chain(right, b21, up, 1)
        chain(right, b21, up, 2)
        second(2)
        chain(right, b21, up, 3)
        mid[...] = dot(right[...], a22[...]).astype(jnp.bfloat16)
        into[3][...] = (b22[...] + dot(mid[...], b12[...])).astype(jnp.bfloat16)
        send(3)
        end(2)
        into[2][...] = dot(right[...], a21[...]).astype(jnp.bfloat16)
        send(2)
        down[...] = dot(b11[...], a22[...]).astype(jnp.bfloat16)
        first(1)
        second(1)
        chain(left, a12, down, 0)
        chain(left, a12, down, 1)
        first(0)
        chain(left, a12, down, 2)
        chain(left, a12, down, 3)
        into[1][...] = dot(left[...], b12[...]).astype(jnp.bfloat16)
        send(1)
        pair_copy(slot, 1, half_rows).start()
        mid[...] = dot(left[...], b11[...]).astype(jnp.bfloat16)
        second(0)
        into[0][...] = (a11[...] + dot(mid[...], a21[...])).astype(jnp.bfloat16)
        send(0)
        pair_copy(slot, 0, half_rows).start()

    def parts(ref):
        return [ref.at[part] for part in range(4)]

    def layer_parts(layer):
        refl, tran, back = [layer_s.at[layer, kind] for kind in range(3)]
        return [refl, tran, tran, back]

    def nothing(*where):
        pass

    last = levels - 1
    assert lay == 2 and nb == 4 and last >= 1
    full_star(
        layer_parts(0), layer_parts(1), 0,
        lambda part: send_far(0, 1, 0, part), nothing, nothing, nothing, nothing,
    )

    slot_end = sum(jnp.where(group >= (1 << k), 1, 0) for k in range(last))
    half = 1 << last

    def one_level(level, distance):
        @pl.when(group >= distance)
        def _():
            full_star(
                parts(land.at[level]), parts(state.at[level]), level + 1,
                lambda part: send_far(level + 1, 2 * distance, level + 1, part),
                functools.partial(relay_first, level),
                functools.partial(relay_second, level),
                functools.partial(relay_end, level),
                lambda: settle(level),
            )

        @pl.when(group < distance)
        def _():
            far_left(level)

            @pl.when(jnp.logical_or(level == 0, 2 * group >= distance))
            def _():
                settle(level)

            @pl.when(level == last - 2)
            def _():
                for part in (3, 2):
                    send_far(last, half, slot_end, part)

            for part in (3, 2):
                @pl.when(jnp.logical_or(level < last - 1, 4 * group >= half))
                def _(part=part):
                    send_far(level + 1, 2 * distance, slot_end, part)
            for part in (1, 0):
                send_far(level + 1, 2 * distance, slot_end, part)

        return 2 * distance

    lax.fori_loop(0, last, one_level, 1)

    @pl.when(group < half)
    def _():
        @pl.when(2 * group >= half)
        def _():
            settle(last)

        for quarter in range(nb):
            out_ref[:, :, cut(quarter)] = state[slot_end, :, own, cut(fixed_place(quarter))]

    def put(part, value):
        for quarter in range(nb):
            out_ref[part, :, cut(quarter)] = value[:, cut(fixed_place(quarter))].astype(
                jnp.bfloat16
            )

    @pl.when(group >= half)
    def _():
        a11, a12, a21, a22 = parts(land.at[last])
        b11, b12, b21, b22 = parts(state.at[last])
        right_rows, left_rows = right.at[:rows], left.at[:rows]
        relay_first(last, 3)
        relay_first(last, 2)
        relay_second(last, 3)
        settle(last)
        relay_end(last, 3)
        up[...] = dot(a22[...], b11[...]).astype(jnp.bfloat16)
        down[...] = dot(b11[...], a22[...]).astype(jnp.bfloat16)
        relay_second(last, 2)
        for piece in range(HALVES):
            far_copy(last, 1, 0, 1, piece).wait_recv()
        for repeat in range(REFL):
            chain(right_rows, b21.at[own], up, repeat)
            chain(left_rows, a12.at[own], down, repeat)
        right_mid = dot(right_rows[...], a22[...]).astype(jnp.bfloat16)
        left_mid = dot(left_rows[...], b11[...]).astype(jnp.bfloat16)
        put(1, dot(left_rows[...], b12[...]))
        put(3, b22[own] + dot(right_mid, b12[...]))
        relay_end(last, 2)
        put(2, dot(right_rows[...], a21[...]))
        for piece in range(HALVES):
            far_copy(last, 1, 0, 0, piece).wait_recv()
        put(0, a11[own] + dot(left_mid, a21[...]))

    for layer in range(lay):
        for_offsets(lambda offset: mode_copy(offset, layer).wait_send())
        share_copy(layer, 0, blk, cross).wait_send()
        share_copy(layer, 1, blk, sib).wait_send()
        share_copy(layer, 2, cross, sib).wait_send()
    for_offsets(lambda offset: aux_copy(offset).wait_send())
    for level in range(levels):
        reach = 1 << level
        sends = group + reach < n
        if level < last:
            sends = jnp.logical_and(sends, group >= reach)

        @pl.when(sends)
        def _(level=level):
            far_left(level)

        @pl.when(group >= reach)
        def _(level=level):
            for part in range(4) if level < last else (2, 3):
                for half in range(HALVES):
                    relay_copy(level, part, half, 0, blk, cross).wait_send()
                    if part >= 2:
                        relay_copy(level, part, half, 1, blk, sib).wait_send()
                        relay_copy(level, part, half, 2, cross, sib).wait_send()

        @pl.when(2 * group >= reach if level else group >= 0)
        def _(level=level):
            for part in range(2):
                pair_copy(level, part, half_rows).wait_send()


def on_device(n, nb, mode_matrix, decay_rate, facet_refl):
    layers, mode_local = decay_rate.shape
    harm = n * mode_matrix.shape[1]
    lay = layers // n
    levels = n.bit_length() - 1
    refl = facet_refl.astype(jnp.float32)
    tran = jnp.sqrt(1.0 - refl * refl) * jnp.exp(-decay_rate.astype(jnp.float32))
    coeff = jnp.concatenate(
        [tran.reshape(n, lay, mode_local), refl.reshape(n, lay, mode_local)], axis=1
    )
    coeff = jnp.pad(coeff, ((0, 0), (0, 8 - 2 * lay), (0, 0)))
    copies = LANES // mode_local
    place = lax.broadcasted_iota(jnp.int32, (1, 1, LANES), 2) // mode_local
    aux = jnp.where(
        place == lax.rem(lax.axis_index("layer"), copies), jnp.tile(coeff, (1, 1, copies)), 0.0
    )
    square = (harm, harm)
    dma = pltpu.SemaphoreType.DMA
    vmem = pl.BlockSpec(memory_space=pltpu.VMEM)
    result = pl.pallas_call(
        functools.partial(stack_kernel, n, nb, levels),
        out_shape=jax.ShapeDtypeStruct((4, harm // nb, harm), jnp.bfloat16),
        in_specs=[vmem, vmem],
        out_specs=vmem,
        scratch_shapes=[
            pltpu.VMEM((nb, lay, n) + mode_matrix.shape[1:], jnp.bfloat16),
            pltpu.VMEM((n, 8, LANES), jnp.float32),
            pltpu.VMEM(square, jnp.bfloat16),
            pltpu.VMEM((2,) + square, jnp.bfloat16),
            pltpu.VMEM((lay, 3) + square, jnp.bfloat16),
            pltpu.VMEM((levels, 4) + square, jnp.bfloat16),
            pltpu.VMEM((levels, 4) + square, jnp.bfloat16),
        ]
        + [pltpu.VMEM(square, jnp.bfloat16)] * 2
        + [pltpu.VMEM((harm // 2, harm), jnp.bfloat16)] * 3
        + [dma((n, lay))] * 2
        + [dma((n,))] * 2
        + [dma((lay, 3))] * 2
        + [dma((levels, 4, HALVES))] * 2
        + [dma((levels, 4, HALVES, 3))] * 2
        + [dma((levels, 2))] * 2,
        compiler_params=pltpu.CompilerParams(
            collective_id=0, has_side_effects=True, vmem_limit_bytes=56 * 1024 * 1024
        ),
        cost_estimate=pl.CostEstimate(
            flops=2 * harm**3 * 60, bytes_accessed=2**20, transcendentals=0
        ),
    )(mode_matrix, aux)
    return result[None]


def solution(mesh):
    n, nb = mesh.shape["layer"], mesh.shape["blk"]
    placed = (P(None, "layer", "blk"), P(None, "layer"), P(None, "layer"))
    return jax.shard_map(
        functools.partial(on_device, n, nb),
        mesh=mesh,
        in_specs=placed,
        out_specs=P("layer", None, "blk", None),
        check_vma=False,
    )
```

```python
import functools

import jax
import jax.numpy as jnp
from jax import lax
from jax.experimental import pallas as pl
from jax.experimental.pallas import tpu as pltpu
from jax.sharding import PartitionSpec as P

REFL = 4
LANES = 128
HALVES = 2
MESH = pl.DeviceIdType.MESH


def dot(left_op, right_op):
    return jnp.dot(left_op, right_op, preferred_element_type=jnp.float32)


def stack_kernel(
    n, nb, levels,
    mode_ref, aux_ref, out_ref,
    mrecv, arecv, modes, scaled, layer_s, state, land,
    down, up, left, right, mid,
    mode_send, mode_recv, aux_send, aux_recv, share_send, share_recv,
    far_send, far_recv, relay_send, relay_recv, join_send, join_recv,
):
    group = lax.axis_index("layer")
    blk = lax.axis_index("blk")
    cross = lax.rem(blk + 2, nb)
    sib = blk + 1 - 2 * lax.rem(blk, 2)
    sib_cross = lax.rem(sib + 2, nb)
    harm = state.shape[-1]
    rows = harm // nb
    lay = mode_ref.shape[0] // n
    mode_local = harm // n

    def cut(index):
        return slice(index * rows, (index + 1) * rows)

    own = pl.ds(pl.multiple_of(blk * rows, rows), rows)

    barrier = pltpu.get_barrier_semaphore()

    def greet(offset, carry):
        pl.semaphore_signal(
            barrier, inc=1, device_id=(lax.rem(group + offset, n), blk), device_id_type=MESH
        )
        return carry

    lax.fori_loop(1, n, greet, 0)
    for other in (cross, sib):
        pl.semaphore_signal(barrier, inc=1, device_id=(group, other), device_id_type=MESH)
    pl.semaphore_wait(barrier, n + 1)

    def mode_copy(offset, layer):
        target = lax.rem(group + offset, n)
        return pltpu.make_async_remote_copy(
            src_ref=mode_ref.at[target * lay + layer],
            dst_ref=mrecv.at[blk, layer, group],
            send_sem=mode_send.at[offset, layer],
            recv_sem=mode_recv.at[offset, layer],
            device_id=(target, blk),
            device_id_type=MESH,
        )

    def aux_copy(offset):
        target = lax.rem(group + offset, n)
        return pltpu.make_async_remote_copy(
            src_ref=aux_ref.at[target],
            dst_ref=arecv.at[group],
            send_sem=aux_send.at[offset],
            recv_sem=aux_recv.at[offset],
            device_id=(target, blk),
            device_id_type=MESH,
        )

    def for_offsets(body):
        def step(offset, carry):
            body(offset)
            return carry

        lax.fori_loop(1, n, step, 0)

    for layer in range(lay):
        for_offsets(lambda offset: mode_copy(offset, layer).start())
        if layer == 0:
            for_offsets(lambda offset: aux_copy(offset).start())
        mrecv[blk, layer, group] = mode_ref[group * lay + layer]
    arecv[group] = aux_ref[group]

    def share_copy(layer, offset, index, piece, other):
        where = mrecv.at[piece, layer, lax.rem(group + n - offset, n)]
        return pltpu.make_async_remote_copy(
            src_ref=where,
            dst_ref=where,
            send_sem=share_send.at[layer, offset, index],
            recv_sem=share_recv.at[layer, offset, index],
            device_id=(group, other),
            device_id_type=MESH,
        )

    def share_first(layer, offset):
        share_copy(layer, offset, 0, blk, cross).start()
        share_copy(layer, offset, 1, blk, sib).start()

    def share_second(layer):
        def step(offset, carry):
            share_copy(layer, offset, 0, cross, cross).wait_recv()
            share_copy(layer, offset, 2, cross, sib).start()
            return carry

        lax.fori_loop(0, n, step, 0)

    def share_end(layer):
        def step(offset, carry):
            share_copy(layer, offset, 1, sib, sib).wait_recv()
            share_copy(layer, offset, 2, sib_cross, sib).wait_recv()
            return carry

        lax.fori_loop(0, n, step, 0)

    def share_left(layer):
        def step(offset, carry):
            share_copy(layer, offset, 0, blk, cross).wait_send()
            share_copy(layer, offset, 1, blk, sib).wait_send()
            share_copy(layer, offset, 2, cross, sib).wait_send()
            return carry

        lax.fori_loop(0, n, step, 0)

    for layer in range(lay):
        share_first(layer, 0)
    for layer in range(lay):
        def pass_on(offset, layer=layer):
            mode_copy(offset, layer).wait_recv()
            share_first(layer, offset)

        for_offsets(pass_on)
    for_offsets(lambda offset: aux_copy(offset).wait_recv())
    per_window = LANES // mode_local
    windows = [
        sum(arecv[index] for index in range(w * per_window, (w + 1) * per_window))
        for w in range(harm // LANES)
    ]

    share_second(0)
    for layer in range(lay):
        share_end(layer)
        if layer + 1 < lay:
            share_second(layer + 1)
        for piece in range(nb):
            cols = cut(piece)
            wide = mrecv[piece, layer].astype(jnp.float32).reshape(harm, rows)
            coeff = windows[piece]
            modes[:, cols] = wide.astype(jnp.bfloat16)
            scaled[0, :, cols] = (wide * coeff[lay + layer][None]).astype(jnp.bfloat16)
            scaled[1, :, cols] = (wide * coeff[layer][None]).astype(jnp.bfloat16)
        for kind in range(2):
            layer_s[layer, kind] = lax.dot_general(
                modes[...], scaled[kind], (((1,), (1,)), ((), ())),
                preferred_element_type=jnp.float32,
            ).astype(jnp.bfloat16)
        layer_s[layer, 2] = -layer_s[layer, 0]

    def piece_rows(quarter, half):
        size = rows // HALVES
        return pl.ds(pl.multiple_of(quarter * rows + half * size, size), size)

    def far_copy(level, distance, slot, part, half):
        return pltpu.make_async_remote_copy(
            src_ref=state.at[slot, part, piece_rows(blk, half)],
            dst_ref=land.at[level, part, piece_rows(blk, half)],
            send_sem=far_send.at[level, part, half],
            recv_sem=far_recv.at[level, part, half],
            device_id=(lax.rem(group + distance, n), blk),
            device_id_type=MESH,
        )

    def send_far(level, distance, slot, part):
        @pl.when(group + distance < n)
        def _():
            for half in range(HALVES):
                far_copy(level, distance, slot, part, half).start()

    def far_left(level):
        for part in range(4):
            for half in range(HALVES):
                far_copy(level, 1, 0, part, half).wait_send()

    def join_copy(slot, part, index, quarter, other):
        where = state.at[slot, part, pl.ds(pl.multiple_of(quarter * rows, rows), rows)]
        return pltpu.make_async_remote_copy(
            src_ref=where,
            dst_ref=where,
            send_sem=join_send.at[slot, part, index],
            recv_sem=join_recv.at[slot, part, index],
            device_id=(group, other),
            device_id_type=MESH,
        )

    def join_first(slot, part):
        join_copy(slot, part, 0, blk, cross).start()
        join_copy(slot, part, 1, blk, sib).start()

    def join_second(slot):
        for part in (1, 0):
            join_copy(slot, part, 0, cross, cross).wait_recv()
            join_copy(slot, part, 2, cross, sib).start()

    def join_end(slot):
        for part in (1, 0):
            join_copy(slot, part, 1, sib, sib).wait_recv()
            join_copy(slot, part, 2, sib_cross, sib).wait_recv()

    def relay_copy(level, part, half, index, piece, other):
        where = land.at[level, part, piece_rows(piece, half)]
        return pltpu.make_async_remote_copy(
            src_ref=where,
            dst_ref=where,
            send_sem=relay_send.at[level, part, half, index],
            recv_sem=relay_recv.at[level, part, half, index],
            device_id=(group, other),
            device_id_type=MESH,
        )

    def relay_first(level, part):
        for half in range(HALVES):
            far_copy(level, 1, 0, part, half).wait_recv()
            if part >= 2:
                relay_copy(level, part, half, 0, blk, cross).start()
                relay_copy(level, part, half, 1, blk, sib).start()

    def relay_second(level, part):
        for half in range(HALVES):
            relay_copy(level, part, half, 0, cross, cross).wait_recv()
            relay_copy(level, part, half, 2, cross, sib).start()

    def relay_end(level, part):
        for half in range(HALVES):
            relay_copy(level, part, half, 1, sib, sib).wait_recv()
            relay_copy(level, part, half, 2, sib_cross, sib).wait_recv()

    def chain(total, start, coupling, repeat):
        source = start if repeat == 0 else total
        total[...] = (start[...] + dot(source[...], coupling[...])).astype(jnp.bfloat16)

    def own_star(upper, lower, put, first, second, end, join):
        a11, a12, a21, a22 = upper
        b11, b12, b21, b22 = lower
        a11, a12, b21, b22 = [ref.at[own] for ref in (a11, a12, b21, b22)]
        first(3)
        join(0)
        second(3)
        join(1)
        end(3)
        up[...] = dot(a22[...], b11[...]).astype(jnp.bfloat16)
        for repeat in range(REFL):
            chain(right, b21, up, repeat)
        mid[...] = dot(right[...], a22[...]).astype(jnp.bfloat16)
        put(3, b22[...] + dot(mid[...], b12[...]))
        down[...] = dot(b11[...], a22[...]).astype(jnp.bfloat16)
        first(1)
        first(2)
        for repeat in range(REFL):
            chain(left, a12, down, repeat)
        put(1, dot(left[...], b12[...]))
        mid[...] = dot(left[...], b11[...]).astype(jnp.bfloat16)
        second(2)
        end(2)
        put(2, dot(right[...], a21[...]))
        first(0)
        put(0, a11[...] + dot(mid[...], a21[...]))

    def parts(ref):
        return [ref.at[part] for part in range(4)]

    def layer_parts(layer):
        refl, tran, back = [layer_s.at[layer, kind] for kind in range(3)]
        return [refl, tran, tran, back]

    def nothing(*where):
        pass

    last = levels - 1
    assert lay == 2 and nb == 4 and last >= 1
    def put_state(level, distance):
        def put(part, value):
            state[level, part, own] = value.astype(jnp.bfloat16)
            send_far(level, distance, level, part)
            if part < 2:
                join_first(level, part)

        return put

    own_star(
        layer_parts(0), layer_parts(1), put_state(0, 1), nothing, nothing, nothing, nothing
    )

    slot_end = sum(jnp.where(group >= (1 << k), 1, 0) for k in range(last))
    half = 1 << last

    def one_level(level, distance):
        @pl.when(group >= distance)
        def _():
            own_star(
                parts(land.at[level]), parts(state.at[level]), put_state(level + 1, 2 * distance),
                functools.partial(relay_first, level),
                functools.partial(relay_second, level),
                functools.partial(relay_end, level),
                lambda step: (join_second, join_end)[step](level),
            )

        @pl.when(group < distance)
        def _():
            @pl.when(jnp.logical_or(level == 0, 2 * group >= distance))
            def _():
                join_second(level)
                join_end(level)

            far_left(level)

            @pl.when(level == last - 2)
            def _():
                for part in (3, 1):
                    send_far(last, half, slot_end, part)

            for part in (3, 1):
                @pl.when(jnp.logical_or(level < last - 1, 4 * group >= half))
                def _(part=part):
                    send_far(level + 1, 2 * distance, slot_end, part)
            for part in (2, 0):
                send_far(level + 1, 2 * distance, slot_end, part)

        return 2 * distance

    lax.fori_loop(0, last, one_level, 1)

    @pl.when(group < half)
    def _():
        @pl.when(2 * group >= half)
        def _():
            join_second(last)
            join_end(last)

        out_ref[...] = state[slot_end, :, own]

    def put_out(part, value):
        out_ref[part] = value.astype(jnp.bfloat16)

    @pl.when(group >= half)
    def _():
        own_star(
            parts(land.at[last]), parts(state.at[last]), put_out,
            functools.partial(relay_first, last),
            functools.partial(relay_second, last),
            functools.partial(relay_end, last),
            lambda step: (join_second, join_end)[step](last),
        )

    for layer in range(lay):
        for_offsets(lambda offset: mode_copy(offset, layer).wait_send())
        share_left(layer)
    for_offsets(lambda offset: aux_copy(offset).wait_send())
    for level in range(levels):
        reach = 1 << level
        sends = group + reach < n
        if level < last:
            sends = jnp.logical_and(sends, group >= reach)

        @pl.when(sends)
        def _(level=level):
            far_left(level)

        @pl.when(group >= reach)
        def _(level=level):
            for part in (2, 3):
                for piece in range(HALVES):
                    relay_copy(level, part, piece, 0, blk, cross).wait_send()
                    relay_copy(level, part, piece, 1, blk, sib).wait_send()
                    relay_copy(level, part, piece, 2, cross, sib).wait_send()

        @pl.when(2 * group >= reach if level else group >= 0)
        def _(level=level):
            for part in range(2):
                join_copy(level, part, 0, blk, cross).wait_send()
                join_copy(level, part, 1, blk, sib).wait_send()
                join_copy(level, part, 2, cross, sib).wait_send()


def on_device(n, nb, mode_matrix, decay_rate, facet_refl):
    layers, mode_local = decay_rate.shape
    harm = n * mode_matrix.shape[1]
    lay = layers // n
    levels = n.bit_length() - 1
    refl = facet_refl.astype(jnp.float32)
    tran = jnp.sqrt(1.0 - refl * refl) * jnp.exp(-decay_rate.astype(jnp.float32))
    coeff = jnp.concatenate(
        [tran.reshape(n, lay, mode_local), refl.reshape(n, lay, mode_local)], axis=1
    )
    coeff = jnp.pad(coeff, ((0, 0), (0, 8 - 2 * lay), (0, 0)))
    copies = LANES // mode_local
    place = lax.broadcasted_iota(jnp.int32, (1, 1, LANES), 2) // mode_local
    aux = jnp.where(
        place == lax.rem(lax.axis_index("layer"), copies), jnp.tile(coeff, (1, 1, copies)), 0.0
    )
    square = (harm, harm)
    dma = pltpu.SemaphoreType.DMA
    vmem = pl.BlockSpec(memory_space=pltpu.VMEM)
    result = pl.pallas_call(
        functools.partial(stack_kernel, n, nb, levels),
        out_shape=jax.ShapeDtypeStruct((4, harm // nb, harm), jnp.bfloat16),
        in_specs=[vmem, vmem],
        out_specs=vmem,
        scratch_shapes=[
            pltpu.VMEM((nb, lay, n) + mode_matrix.shape[1:], jnp.bfloat16),
            pltpu.VMEM((n, 8, LANES), jnp.float32),
            pltpu.VMEM(square, jnp.bfloat16),
            pltpu.VMEM((2,) + square, jnp.bfloat16),
            pltpu.VMEM((lay, 3) + square, jnp.bfloat16),
            pltpu.VMEM((levels, 4) + square, jnp.bfloat16),
            pltpu.VMEM((levels, 4) + square, jnp.bfloat16),
        ]
        + [pltpu.VMEM(square, jnp.bfloat16)] * 2
        + [pltpu.VMEM((harm // nb, harm), jnp.bfloat16)] * 3
        + [dma((n, lay))] * 2
        + [dma((n,))] * 2
        + [dma((lay, n, 3))] * 2
        + [dma((levels, 4, HALVES))] * 2
        + [dma((levels, 4, HALVES, 3))] * 2
        + [dma((levels, 2, 3))] * 2,
        compiler_params=pltpu.CompilerParams(
            collective_id=0, has_side_effects=True, vmem_limit_bytes=56 * 1024 * 1024
        ),
        cost_estimate=pl.CostEstimate(
            flops=2 * harm**3 * 60, bytes_accessed=2**20, transcendentals=0
        ),
    )(mode_matrix, aux)
    return result[None]


def solution(mesh):
    n, nb = mesh.shape["layer"], mesh.shape["blk"]
    placed = (P(None, "layer", "blk"), P(None, "layer"), P(None, "layer"))
    return jax.shard_map(
        functools.partial(on_device, n, nb),
        mesh=mesh,
        in_specs=placed,
        out_specs=P("layer", None, "blk", None),
        check_vma=False,
    )
```

```python
import functools

import jax
import jax.numpy as jnp
from jax import lax
from jax.experimental import pallas as pl
from jax.experimental.pallas import tpu as pltpu
from jax.sharding import PartitionSpec as P

REFL = 4
LANES = 128
HALVES = 2
MESH = pl.DeviceIdType.MESH


def dot(left_op, right_op):
    return jnp.dot(left_op, right_op, preferred_element_type=jnp.float32)


def stack_kernel(
    n, nb, levels,
    mode_ref, aux_ref, out_ref,
    mrecv, arecv, modes, scaled, layer_s, state, land,
    down, up, left, right, mid,
    mode_send, mode_recv, aux_send, aux_recv, share_send, share_recv,
    far_send, far_recv, relay_send, relay_recv, join_send, join_recv,
):
    group = lax.axis_index("layer")
    blk = lax.axis_index("blk")
    cross = lax.rem(blk + 2, nb)
    sib = blk + 1 - 2 * lax.rem(blk, 2)
    sib_cross = lax.rem(sib + 2, nb)
    harm = state.shape[-1]
    rows = harm // nb
    lay = mode_ref.shape[0] // n
    last = levels - 1
    half = 1 << last
    quarter = half // 2
    middle = jnp.logical_and(group >= half, group < half + quarter)
    mode_local = harm // n

    def cut(index):
        return slice(index * rows, (index + 1) * rows)

    own = pl.ds(pl.multiple_of(blk * rows, rows), rows)

    barrier = pltpu.get_barrier_semaphore()

    def greet(offset, carry):
        pl.semaphore_signal(
            barrier, inc=1, device_id=(lax.rem(group + offset, n), blk), device_id_type=MESH
        )
        return carry

    lax.fori_loop(1, n, greet, 0)
    for other in (cross, sib):
        pl.semaphore_signal(barrier, inc=1, device_id=(group, other), device_id_type=MESH)
    pl.semaphore_wait(barrier, n + 1)

    def mode_copy(offset, layer):
        target = lax.rem(group + offset, n)
        return pltpu.make_async_remote_copy(
            src_ref=mode_ref.at[target * lay + layer],
            dst_ref=mrecv.at[blk, layer, group],
            send_sem=mode_send.at[offset, layer],
            recv_sem=mode_recv.at[offset, layer],
            device_id=(target, blk),
            device_id_type=MESH,
        )

    def aux_copy(offset):
        target = lax.rem(group + offset, n)
        return pltpu.make_async_remote_copy(
            src_ref=aux_ref.at[target],
            dst_ref=arecv.at[group],
            send_sem=aux_send.at[offset],
            recv_sem=aux_recv.at[offset],
            device_id=(target, blk),
            device_id_type=MESH,
        )

    def for_offsets(body):
        def step(offset, carry):
            body(offset)
            return carry

        lax.fori_loop(1, n, step, 0)

    for layer in range(lay):
        for_offsets(lambda offset: mode_copy(offset, layer).start())
        if layer == 0:
            for_offsets(lambda offset: aux_copy(offset).start())
        mrecv[blk, layer, group] = mode_ref[group * lay + layer]
    arecv[group] = aux_ref[group]

    def share_copy(layer, offset, index, piece, other):
        where = mrecv.at[piece, layer, lax.rem(group + n - offset, n)]
        return pltpu.make_async_remote_copy(
            src_ref=where,
            dst_ref=where,
            send_sem=share_send.at[layer, offset, index],
            recv_sem=share_recv.at[layer, offset, index],
            device_id=(group, other),
            device_id_type=MESH,
        )

    def share_first(layer, offset):
        share_copy(layer, offset, 0, blk, cross).start()
        share_copy(layer, offset, 1, blk, sib).start()

    def share_second(layer):
        def step(offset, carry):
            share_copy(layer, offset, 0, cross, cross).wait_recv()
            share_copy(layer, offset, 2, cross, sib).start()
            return carry

        lax.fori_loop(0, n, step, 0)

    def share_end(layer):
        def step(offset, carry):
            share_copy(layer, offset, 1, sib, sib).wait_recv()
            share_copy(layer, offset, 2, sib_cross, sib).wait_recv()
            return carry

        lax.fori_loop(0, n, step, 0)

    def share_left(layer):
        def step(offset, carry):
            share_copy(layer, offset, 0, blk, cross).wait_send()
            share_copy(layer, offset, 1, blk, sib).wait_send()
            share_copy(layer, offset, 2, cross, sib).wait_send()
            return carry

        lax.fori_loop(0, n, step, 0)

    for layer in range(lay):
        share_first(layer, 0)
    for layer in range(lay):
        def pass_on(offset, layer=layer):
            mode_copy(offset, layer).wait_recv()
            share_first(layer, offset)

        for_offsets(pass_on)
    for_offsets(lambda offset: aux_copy(offset).wait_recv())
    per_window = LANES // mode_local
    windows = [
        sum(arecv[index] for index in range(w * per_window, (w + 1) * per_window))
        for w in range(harm // LANES)
    ]

    share_second(0)
    for layer in range(lay):
        share_end(layer)
        if layer + 1 < lay:
            share_second(layer + 1)
        for piece in range(nb):
            cols = cut(piece)
            wide = mrecv[piece, layer].astype(jnp.float32).reshape(harm, rows)
            coeff = windows[piece]
            modes[:, cols] = wide.astype(jnp.bfloat16)
            scaled[0, :, cols] = (wide * coeff[lay + layer][None]).astype(jnp.bfloat16)
            scaled[1, :, cols] = (wide * coeff[layer][None]).astype(jnp.bfloat16)
        for kind in range(2):
            layer_s[layer, kind] = lax.dot_general(
                modes[...], scaled[kind], (((1,), (1,)), ((), ())),
                preferred_element_type=jnp.float32,
            ).astype(jnp.bfloat16)
        layer_s[layer, 2] = -layer_s[layer, 0]

    def piece_rows(quarter, half):
        size = rows // HALVES
        return pl.ds(pl.multiple_of(quarter * rows + half * size, size), size)

    def far_copy(level, distance, slot, part, half):
        return pltpu.make_async_remote_copy(
            src_ref=state.at[slot, part, piece_rows(blk, half)],
            dst_ref=land.at[level, part, piece_rows(blk, half)],
            send_sem=far_send.at[level, part, half],
            recv_sem=far_recv.at[level, part, half],
            device_id=(lax.rem(group + distance, n), blk),
            device_id_type=MESH,
        )

    def start_far(level, distance, slot, part):
        for half in range(HALVES):
            far_copy(level, distance, slot, part, half).start()

    def send_far(level, distance, slot, part):
        sends = jnp.logical_and(
            group + distance < n, jnp.logical_or(level != last, group < quarter)
        )
        pl.when(sends)(lambda: start_far(level, distance, slot, part))

    def far_left(level):
        for part in range(4):
            for half in range(HALVES):
                far_copy(level, 1, 0, part, half).wait_send()

    def join_copy(slot, part, index, quarter, other):
        where = state.at[slot, part, pl.ds(pl.multiple_of(quarter * rows, rows), rows)]
        return pltpu.make_async_remote_copy(
            src_ref=where,
            dst_ref=where,
            send_sem=join_send.at[slot, part, index],
            recv_sem=join_recv.at[slot, part, index],
            device_id=(group, other),
            device_id_type=MESH,
        )

    def join_first(slot, part):
        join_copy(slot, part, 0, blk, cross).start()
        join_copy(slot, part, 1, blk, sib).start()

    def join_second(slot):
        for part in (1, 0):
            join_copy(slot, part, 0, cross, cross).wait_recv()
            join_copy(slot, part, 2, cross, sib).start()

    def join_end(slot):
        for part in (1, 0):
            join_copy(slot, part, 1, sib, sib).wait_recv()
            join_copy(slot, part, 2, sib_cross, sib).wait_recv()

    def relay_copy(level, part, half, index, piece, other):
        where = land.at[level, part, piece_rows(piece, half)]
        return pltpu.make_async_remote_copy(
            src_ref=where,
            dst_ref=where,
            send_sem=relay_send.at[level, part, half, index],
            recv_sem=relay_recv.at[level, part, half, index],
            device_id=(group, other),
            device_id_type=MESH,
        )

    def relay_first(level, part, near=None):
        for half in range(HALVES):
            far_copy(level, 1, 0, part, half).wait_recv()

            def pass_on(half=half):
                relay_copy(level, part, half, 0, blk, cross).start()
                relay_copy(level, part, half, 1, blk, sib).start()

            if part >= 2:
                pass_on()
            elif near is not None:
                pl.when(near)(pass_on)

    def relay_second(level, part):
        for half in range(HALVES):
            relay_copy(level, part, half, 0, cross, cross).wait_recv()
            relay_copy(level, part, half, 2, cross, sib).start()

    def relay_end(level, part):
        for half in range(HALVES):
            relay_copy(level, part, half, 1, sib, sib).wait_recv()
            relay_copy(level, part, half, 2, sib_cross, sib).wait_recv()

    def chain(total, start, coupling, repeat):
        source = start if repeat == 0 else total
        total[...] = (start[...] + dot(source[...], coupling[...])).astype(jnp.bfloat16)

    def own_star(upper, lower, put, first, second, end, join):
        a11, a12, a21, a22 = upper
        b11, b12, b21, b22 = lower
        a11, a12, b21, b22 = [ref.at[own] for ref in (a11, a12, b21, b22)]
        first(3)
        join(0)
        second(3)
        join(1)
        end(3)
        up[...] = dot(a22[...], b11[...]).astype(jnp.bfloat16)
        for repeat in range(REFL):
            chain(right, b21, up, repeat)
        mid[...] = dot(right[...], a22[...]).astype(jnp.bfloat16)
        put(3, b22[...] + dot(mid[...], b12[...]))
        down[...] = dot(b11[...], a22[...]).astype(jnp.bfloat16)
        first(1)
        first(2)
        for repeat in range(REFL):
            chain(left, a12, down, repeat)
        put(1, dot(left[...], b12[...]))
        mid[...] = dot(left[...], b11[...]).astype(jnp.bfloat16)
        second(2)
        end(2)
        put(2, dot(right[...], a21[...]))
        first(0)
        put(0, a11[...] + dot(mid[...], a21[...]))

    def parts(ref):
        return [ref.at[part] for part in range(4)]

    def layer_parts(layer):
        refl, tran, back = [layer_s.at[layer, kind] for kind in range(3)]
        return [refl, tran, tran, back]

    def nothing(*where):
        pass

    assert lay == 2 and nb == 4 and last >= 2
    def put_state(level, distance):
        def put(part, value):
            state[level, part, own] = value.astype(jnp.bfloat16)
            send_far(level, distance, level, part)
            if part < 2:
                join_first(level, part)

        return put

    own_star(
        layer_parts(0), layer_parts(1), put_state(0, 1), nothing, nothing, nothing, nothing
    )

    slot_end = sum(jnp.where(group >= (1 << k), 1, 0) for k in range(last))

    def one_level(level, distance):
        @pl.when(group >= distance)
        def _():
            own_star(
                parts(land.at[level]), parts(state.at[level]), put_state(level + 1, 2 * distance),
                functools.partial(
                    relay_first, level, near=jnp.logical_and(level == last - 1, middle)
                ),
                functools.partial(relay_second, level),
                functools.partial(relay_end, level),
                lambda step: (join_second, join_end)[step](level),
            )

        @pl.when(group < distance)
        def _():
            @pl.when(jnp.logical_or(level == 0, 2 * group >= distance))
            def _():
                join_second(level)
                join_end(level)

            far_left(level)

            @pl.when(level == last - 2)
            def _():
                for part in (3, 1):
                    send_far(last, half, slot_end, part)

            for part in (3, 1):
                @pl.when(jnp.logical_or(level < last - 1, 4 * group >= half))
                def _(part=part):
                    send_far(level + 1, 2 * distance, slot_end, part)
            for part in (2, 0):
                send_far(level + 1, 2 * distance, slot_end, part)

        return 2 * distance

    lax.fori_loop(0, last, one_level, 1)

    @pl.when(middle)
    def _():
        def near_join(step):
            for part in (1, 0):
                (relay_second, relay_end)[step](last - 1, part)

        def put_on(part, value):
            state[levels, part, own] = value.astype(jnp.bfloat16)
            start_far(last, quarter, levels, part)

        own_star(
            parts(land.at[last]), parts(land.at[last - 1]), put_on,
            functools.partial(relay_first, last),
            functools.partial(relay_second, last),
            functools.partial(relay_end, last),
            near_join,
        )

    def unless_middle(act):
        return lambda part: pl.when(jnp.logical_not(middle))(lambda: act(last, part))

    @pl.when(group < half)
    def _():
        @pl.when(2 * group >= half)
        def _():
            join_second(last)
            join_end(last)

        out_ref[...] = state[slot_end, :, own]

    def put_out(part, value):
        out_ref[part] = value.astype(jnp.bfloat16)

    @pl.when(group >= half)
    def _():
        own_star(
            parts(land.at[last]), parts(state.at[last]), put_out,
            unless_middle(relay_first),
            unless_middle(relay_second),
            unless_middle(relay_end),
            lambda step: (join_second, join_end)[step](last),
        )

    for layer in range(lay):
        for_offsets(lambda offset: mode_copy(offset, layer).wait_send())
        share_left(layer)
    for_offsets(lambda offset: aux_copy(offset).wait_send())
    for level in range(levels):
        reach = 1 << level
        sends = group + reach < n
        if level < last:
            sends = jnp.logical_and(sends, group >= reach)
        else:
            sends = jnp.logical_or(group < quarter, middle)

        @pl.when(sends)
        def _(level=level):
            far_left(level)

        @pl.when(group >= reach)
        def _(level=level):
            for part in (2, 3):
                for piece in range(HALVES):
                    relay_copy(level, part, piece, 0, blk, cross).wait_send()
                    relay_copy(level, part, piece, 1, blk, sib).wait_send()
                    relay_copy(level, part, piece, 2, cross, sib).wait_send()

        if level == last - 1:
            @pl.when(middle)
            def _(level=level):
                for part in range(2):
                    for piece in range(HALVES):
                        relay_copy(level, part, piece, 0, blk, cross).wait_send()
                        relay_copy(level, part, piece, 1, blk, sib).wait_send()
                        relay_copy(level, part, piece, 2, cross, sib).wait_send()

        @pl.when(2 * group >= reach if level else group >= 0)
        def _(level=level):
            for part in range(2):
                join_copy(level, part, 0, blk, cross).wait_send()
                join_copy(level, part, 1, blk, sib).wait_send()
                join_copy(level, part, 2, cross, sib).wait_send()


def on_device(n, nb, mode_matrix, decay_rate, facet_refl):
    layers, mode_local = decay_rate.shape
    harm = n * mode_matrix.shape[1]
    lay = layers // n
    levels = n.bit_length() - 1
    refl = facet_refl.astype(jnp.float32)
    tran = jnp.sqrt(1.0 - refl * refl) * jnp.exp(-decay_rate.astype(jnp.float32))
    coeff = jnp.concatenate(
        [tran.reshape(n, lay, mode_local), refl.reshape(n, lay, mode_local)], axis=1
    )
    coeff = jnp.pad(coeff, ((0, 0), (0, 8 - 2 * lay), (0, 0)))
    copies = LANES // mode_local
    place = lax.broadcasted_iota(jnp.int32, (1, 1, LANES), 2) // mode_local
    aux = jnp.where(
        place == lax.rem(lax.axis_index("layer"), copies), jnp.tile(coeff, (1, 1, copies)), 0.0
    )
    square = (harm, harm)
    dma = pltpu.SemaphoreType.DMA
    vmem = pl.BlockSpec(memory_space=pltpu.VMEM)
    result = pl.pallas_call(
        functools.partial(stack_kernel, n, nb, levels),
        out_shape=jax.ShapeDtypeStruct((4, harm // nb, harm), jnp.bfloat16),
        in_specs=[vmem, vmem],
        out_specs=vmem,
        scratch_shapes=[
            pltpu.VMEM((nb, lay, n) + mode_matrix.shape[1:], jnp.bfloat16),
            pltpu.VMEM((n, 8, LANES), jnp.float32),
            pltpu.VMEM(square, jnp.bfloat16),
            pltpu.VMEM((2,) + square, jnp.bfloat16),
            pltpu.VMEM((lay, 3) + square, jnp.bfloat16),
            pltpu.VMEM((levels + 1, 4) + square, jnp.bfloat16),
            pltpu.VMEM((levels, 4) + square, jnp.bfloat16),
        ]
        + [pltpu.VMEM(square, jnp.bfloat16)] * 2
        + [pltpu.VMEM((harm // nb, harm), jnp.bfloat16)] * 3
        + [dma((n, lay))] * 2
        + [dma((n,))] * 2
        + [dma((lay, n, 3))] * 2
        + [dma((levels, 4, HALVES))] * 2
        + [dma((levels, 4, HALVES, 3))] * 2
        + [dma((levels, 2, 3))] * 2,
        compiler_params=pltpu.CompilerParams(
            collective_id=0, has_side_effects=True, vmem_limit_bytes=56 * 1024 * 1024
        ),
        cost_estimate=pl.CostEstimate(
            flops=2 * harm**3 * 60, bytes_accessed=2**20, transcendentals=0
        ),
    )(mode_matrix, aux)
    return result[None]


def solution(mesh):
    n, nb = mesh.shape["layer"], mesh.shape["blk"]
    placed = (P(None, "layer", "blk"), P(None, "layer"), P(None, "layer"))
    return jax.shard_map(
        functools.partial(on_device, n, nb),
        mesh=mesh,
        in_specs=placed,
        out_specs=P("layer", None, "blk", None),
        check_vma=False,
    )
```

```python
import functools

import jax
import jax.numpy as jnp
from jax import lax
from jax.experimental import pallas as pl
from jax.experimental.pallas import tpu as pltpu
from jax.sharding import PartitionSpec as P

REFL = 4
LANES = 128
HALVES = 2
MESH = pl.DeviceIdType.MESH


def dot(left_op, right_op):
    return jnp.dot(left_op, right_op, preferred_element_type=jnp.float32)


def stack_kernel(
    n, nb, levels,
    mode_ref, aux_ref, out_ref,
    mrecv, arecv, modes, scaled, layer_s, state, land,
    up, total, mid,
    mode_send, mode_recv, aux_send, aux_recv, share_send, share_recv,
    far_send, far_recv, relay_send, relay_recv, join_send, join_recv,
    swap_send, swap_recv,
):
    group = lax.axis_index("layer")
    blk = lax.axis_index("blk")
    cross = lax.rem(blk + 2, nb)
    sib = blk + 1 - 2 * lax.rem(blk, 2)
    sib_cross = lax.rem(sib + 2, nb)
    harm = state.shape[-1]
    rows = harm // nb
    lay = mode_ref.shape[0] // n
    mode_local = harm // n

    def cut(index):
        return slice(index * rows, (index + 1) * rows)

    role = lax.rem(blk, 2)
    lead_part, next_part = 3 - 2 * role, 2 - 2 * role
    own = pl.ds(pl.multiple_of(blk * rows, rows), rows)
    sib_own = pl.ds(pl.multiple_of(sib * rows, rows), rows)
    wing = 2 * rows

    def wing_of(device):
        return pl.ds(pl.multiple_of(lax.div(device, 2) * wing, wing), wing)

    mine = wing_of(blk)

    barrier = pltpu.get_barrier_semaphore()

    def greet(offset, carry):
        pl.semaphore_signal(
            barrier, inc=1, device_id=(lax.rem(group + offset, n), blk), device_id_type=MESH
        )
        return carry

    lax.fori_loop(1, n, greet, 0)
    for other in (cross, sib):
        pl.semaphore_signal(barrier, inc=1, device_id=(group, other), device_id_type=MESH)
    pl.semaphore_wait(barrier, n + 1)

    def mode_copy(offset, layer):
        target = lax.rem(group + offset, n)
        return pltpu.make_async_remote_copy(
            src_ref=mode_ref.at[target * lay + layer],
            dst_ref=mrecv.at[blk, layer, group],
            send_sem=mode_send.at[offset, layer],
            recv_sem=mode_recv.at[offset, layer],
            device_id=(target, blk),
            device_id_type=MESH,
        )

    def aux_copy(offset):
        target = lax.rem(group + offset, n)
        return pltpu.make_async_remote_copy(
            src_ref=aux_ref.at[target],
            dst_ref=arecv.at[group],
            send_sem=aux_send.at[offset],
            recv_sem=aux_recv.at[offset],
            device_id=(target, blk),
            device_id_type=MESH,
        )

    def for_offsets(body):
        def step(offset, carry):
            body(offset)
            return carry

        lax.fori_loop(1, n, step, 0)

    for layer in range(lay):
        for_offsets(lambda offset: mode_copy(offset, layer).start())
        if layer == 0:
            for_offsets(lambda offset: aux_copy(offset).start())
        mrecv[blk, layer, group] = mode_ref[group * lay + layer]
    arecv[group] = aux_ref[group]

    def share_copy(layer, offset, index, piece, other):
        where = mrecv.at[piece, layer, lax.rem(group + n - offset, n)]
        return pltpu.make_async_remote_copy(
            src_ref=where,
            dst_ref=where,
            send_sem=share_send.at[layer, offset, index],
            recv_sem=share_recv.at[layer, offset, index],
            device_id=(group, other),
            device_id_type=MESH,
        )

    def share_first(layer, offset):
        share_copy(layer, offset, 0, blk, cross).start()
        share_copy(layer, offset, 1, blk, sib).start()

    def share_second(layer):
        def step(offset, carry):
            share_copy(layer, offset, 0, cross, cross).wait_recv()
            share_copy(layer, offset, 2, cross, sib).start()
            return carry

        lax.fori_loop(0, n, step, 0)

    def share_end(layer):
        def step(offset, carry):
            share_copy(layer, offset, 1, sib, sib).wait_recv()
            share_copy(layer, offset, 2, sib_cross, sib).wait_recv()
            return carry

        lax.fori_loop(0, n, step, 0)

    def share_left(layer):
        def step(offset, carry):
            share_copy(layer, offset, 0, blk, cross).wait_send()
            share_copy(layer, offset, 1, blk, sib).wait_send()
            share_copy(layer, offset, 2, cross, sib).wait_send()
            return carry

        lax.fori_loop(0, n, step, 0)

    for layer in range(lay):
        share_first(layer, 0)
    for layer in range(lay):
        def pass_on(offset, layer=layer):
            mode_copy(offset, layer).wait_recv()
            share_first(layer, offset)

        for_offsets(pass_on)
    for_offsets(lambda offset: aux_copy(offset).wait_recv())
    per_window = LANES // mode_local
    windows = [
        sum(arecv[index] for index in range(w * per_window, (w + 1) * per_window))
        for w in range(harm // LANES)
    ]

    share_second(0)
    for layer in range(lay):
        share_end(layer)
        if layer + 1 < lay:
            share_second(layer + 1)
        for piece in range(nb):
            cols = cut(piece)
            wide = mrecv[piece, layer].astype(jnp.float32).reshape(harm, rows)
            coeff = windows[piece]
            modes[:, cols] = wide.astype(jnp.bfloat16)
            scaled[0, :, cols] = (wide * coeff[lay + layer][None]).astype(jnp.bfloat16)
            scaled[1, :, cols] = (wide * coeff[layer][None]).astype(jnp.bfloat16)
        for kind in range(2):
            layer_s[layer, kind] = lax.dot_general(
                modes[...], scaled[kind], (((1,), (1,)), ((), ())),
                preferred_element_type=jnp.float32,
            ).astype(jnp.bfloat16)
        layer_s[layer, 2] = -layer_s[layer, 0]

    def piece_rows(device, half):
        size = wing // HALVES
        return pl.ds(pl.multiple_of(lax.div(device, 2) * wing + half * size, size), size)

    def far_copy(level, distance, slot, part, half):
        return pltpu.make_async_remote_copy(
            src_ref=state.at[slot, part, piece_rows(blk, half)],
            dst_ref=land.at[level, part, piece_rows(blk, half)],
            send_sem=far_send.at[level, part, half],
            recv_sem=far_recv.at[level, part, half],
            device_id=(lax.rem(group + distance, n), blk),
            device_id_type=MESH,
        )

    def send_far(level, distance, slot, part):
        @pl.when(group + distance < n)
        def _():
            for half in range(HALVES):
                far_copy(level, distance, slot, part, half).start()

    def far_left(level):
        for part in (lead_part, next_part):
            for half in range(HALVES):
                far_copy(level, 1, 0, part, half).wait_send()

    def far_end(level, part):
        for half in range(HALVES):
            far_copy(level, 1, 0, part, half).wait_recv()

    def join_copy(slot, part, index, device, other):
        where = state.at[slot, part, wing_of(device)]
        return pltpu.make_async_remote_copy(
            src_ref=where,
            dst_ref=where,
            send_sem=join_send.at[slot, part, index],
            recv_sem=join_recv.at[slot, part, index],
            device_id=(group, other),
            device_id_type=MESH,
        )

    def join_first(slot, part):
        join_copy(slot, part, 0, blk, cross).start()
        join_copy(slot, part, 1, blk, sib).start()

    def join_second(slot):
        for part in (1, 0):
            join_copy(slot, part, 0, cross, cross).wait_recv()
            join_copy(slot, part, 2, cross, sib).start()

    def join_end(slot):
        for part in (1, 0):
            join_copy(slot, part, 1, sib, sib).wait_recv()
            join_copy(slot, part, 2, sib_cross, sib).wait_recv()

    def join(slot):
        pl.when(role == 1)(lambda: join_second(slot))
        pl.when(role == 0)(lambda: join_end(slot))

    def relay_copy(level, part, half, index, device, other):
        where = land.at[level, part, piece_rows(device, half)]
        return pltpu.make_async_remote_copy(
            src_ref=where,
            dst_ref=where,
            send_sem=relay_send.at[level, part, half, index],
            recv_sem=relay_recv.at[level, part, half, index],
            device_id=(group, other),
            device_id_type=MESH,
        )

    def relay_first(level, part):
        for half in range(HALVES):
            far_copy(level, 1, 0, part, half).wait_recv()
            relay_copy(level, part, half, 0, blk, cross).start()
            relay_copy(level, part, half, 1, blk, sib).start()

    def relay_second(level, part):
        for half in range(HALVES):
            relay_copy(level, part, half, 0, cross, cross).wait_recv()
            relay_copy(level, part, half, 2, cross, sib).start()

    def relay_end(level, part):
        for half in range(HALVES):
            relay_copy(level, part, half, 1, sib, sib).wait_recv()
            relay_copy(level, part, half, 2, sib_cross, sib).wait_recv()

    def swap_copy(slot, part):
        return pltpu.make_async_remote_copy(
            src_ref=state.at[slot, part, sib_own],
            dst_ref=out_ref.at[part],
            send_sem=swap_send.at[part],
            recv_sem=swap_recv.at[part],
            device_id=(group, sib),
            device_id_type=MESH,
        )

    def put_out(slot, part):
        swap_copy(slot, part).start()
        out_ref[part] = state[slot, part, own]

    def chain(total, start, coupling, repeat):
        source = start if repeat == 0 else total
        total[...] = (start[...] + dot(source[...], coupling[...])).astype(jnp.bfloat16)

    def under_star(upper, lower, put, level):
        a11, a12, a21, a22 = upper
        b11, b12, b21, b22 = lower
        b21, b22 = b21.at[mine], b22.at[mine]
        if level is not None:
            relay_first(level, 3)
            join_end(level)
            relay_second(level, 3)
        up[...] = dot(a22[...], b11[...]).astype(jnp.bfloat16)
        chain(total, b21, up, 0)
        chain(total, b21, up, 1)
        if level is not None:
            relay_first(level, 2)
        chain(total, b21, up, 2)
        chain(total, b21, up, 3)
        mid[...] = dot(total[...], a22[...]).astype(jnp.bfloat16)
        put(3, b22[...] + dot(mid[...], b12[...]))
        if level is not None:
            relay_second(level, 2)
        put(2, dot(total[...], a21[...]))

    def over_star(upper, lower, put, level):
        a11, a12, a21, a22 = upper
        b11, b12, b21, b22 = lower
        a11, a12 = a11.at[mine], a12.at[mine]
        if level is not None:
            join_second(level)
            relay_end(level, 3)
        up[...] = dot(b11[...], a22[...]).astype(jnp.bfloat16)
        if level is not None:
            far_end(level, 1)
        for repeat in range(REFL):
            chain(total, a12, up, repeat)
        put(1, dot(total[...], b12[...]))
        mid[...] = dot(total[...], b11[...]).astype(jnp.bfloat16)
        if level is not None:
            far_end(level, 0)
            relay_end(level, 2)
        put(0, a11[...] + dot(mid[...], a21[...]))

    def star(upper, lower, put, level):
        pl.when(role == 0)(lambda: under_star(upper, lower, put, level))
        pl.when(role == 1)(lambda: over_star(upper, lower, put, level))

    def parts(ref):
        return [ref.at[part] for part in range(4)]

    def layer_parts(layer):
        refl, tran, back = [layer_s.at[layer, kind] for kind in range(3)]
        return [refl, tran, tran, back]

    last = levels - 1
    assert lay == 2 and nb == 4 and last >= 1

    def put_state(level, distance):
        def put(part, value):
            state[level, part, mine] = value.astype(jnp.bfloat16)
            send_far(level, distance, level, part)
            if part < 2:
                join_first(level, part)

        return put

    star(layer_parts(0), layer_parts(1), put_state(0, 1), None)

    slot_end = sum(jnp.where(group >= (1 << k), 1, 0) for k in range(last))
    half = 1 << last

    def one_level(level, distance):
        @pl.when(group >= distance)
        def _():
            star(
                parts(land.at[level]), parts(state.at[level]),
                put_state(level + 1, 2 * distance), level,
            )

        @pl.when(group < distance)
        def _():
            @pl.when(jnp.logical_or(level == 0, 2 * group >= distance))
            def _():
                join(level)

            far_left(level)

            @pl.when(level == last - 2)
            def _():
                send_far(last, half, slot_end, lead_part)

            @pl.when(jnp.logical_or(level < last - 1, 4 * group >= half))
            def _():
                send_far(level + 1, 2 * distance, slot_end, lead_part)

            send_far(level + 1, 2 * distance, slot_end, next_part)

        return 2 * distance

    lax.fori_loop(0, last, one_level, 1)

    @pl.when(group < half)
    def _():
        @pl.when(2 * group >= half)
        def _():
            join(last)

        put_out(slot_end, lead_part)
        put_out(slot_end, next_part)

    def put_last(part, value):
        state[levels, part, mine] = value.astype(jnp.bfloat16)
        put_out(levels, part)

    @pl.when(group >= half)
    def _():
        star(parts(land.at[last]), parts(state.at[last]), put_last, last)

    for part in (3 - lead_part, 3 - next_part):
        swap_copy(0, part).wait_recv()

    for layer in range(lay):
        for_offsets(lambda offset: mode_copy(offset, layer).wait_send())
        share_left(layer)
    for_offsets(lambda offset: aux_copy(offset).wait_send())
    for level in range(levels):
        reach = 1 << level
        sends = group + reach < n
        if level < last:
            sends = jnp.logical_and(sends, group >= reach)

        @pl.when(sends)
        def _(level=level):
            far_left(level)

        @pl.when(jnp.logical_and(group >= reach, role == 0))
        def _(level=level):
            for part in (2, 3):
                for piece in range(HALVES):
                    relay_copy(level, part, piece, 0, blk, cross).wait_send()
                    relay_copy(level, part, piece, 1, blk, sib).wait_send()
                    relay_copy(level, part, piece, 2, cross, sib).wait_send()

        formed = 2 * group >= reach if level else group >= 0

        @pl.when(jnp.logical_and(formed, role == 1))
        def _(level=level):
            for part in range(2):
                join_copy(level, part, 0, blk, cross).wait_send()
                join_copy(level, part, 1, blk, sib).wait_send()
                join_copy(level, part, 2, cross, sib).wait_send()

    for part in (lead_part, next_part):
        swap_copy(0, part).wait_send()


def on_device(n, nb, mode_matrix, decay_rate, facet_refl):
    layers, mode_local = decay_rate.shape
    harm = n * mode_matrix.shape[1]
    lay = layers // n
    levels = n.bit_length() - 1
    refl = facet_refl.astype(jnp.float32)
    tran = jnp.sqrt(1.0 - refl * refl) * jnp.exp(-decay_rate.astype(jnp.float32))
    coeff = jnp.concatenate(
        [tran.reshape(n, lay, mode_local), refl.reshape(n, lay, mode_local)], axis=1
    )
    coeff = jnp.pad(coeff, ((0, 0), (0, 8 - 2 * lay), (0, 0)))
    copies = LANES // mode_local
    place = lax.broadcasted_iota(jnp.int32, (1, 1, LANES), 2) // mode_local
    aux = jnp.where(
        place == lax.rem(lax.axis_index("layer"), copies), jnp.tile(coeff, (1, 1, copies)), 0.0
    )
    square = (harm, harm)
    dma = pltpu.SemaphoreType.DMA
    vmem = pl.BlockSpec(memory_space=pltpu.VMEM)
    result = pl.pallas_call(
        functools.partial(stack_kernel, n, nb, levels),
        out_shape=jax.ShapeDtypeStruct((4, harm // nb, harm), jnp.bfloat16),
        in_specs=[vmem, vmem],
        out_specs=vmem,
        scratch_shapes=[
            pltpu.VMEM((nb, lay, n) + mode_matrix.shape[1:], jnp.bfloat16),
            pltpu.VMEM((n, 8, LANES), jnp.float32),
            pltpu.VMEM(square, jnp.bfloat16),
            pltpu.VMEM((2,) + square, jnp.bfloat16),
            pltpu.VMEM((lay, 3) + square, jnp.bfloat16),
            pltpu.VMEM((levels + 1, 4) + square, jnp.bfloat16),
            pltpu.VMEM((levels, 4) + square, jnp.bfloat16),
        ]
        + [pltpu.VMEM(square, jnp.bfloat16)]
        + [pltpu.VMEM((harm // 2, harm), jnp.bfloat16)] * 2
        + [dma((n, lay))] * 2
        + [dma((n,))] * 2
        + [dma((lay, n, 3))] * 2
        + [dma((levels, 4, HALVES))] * 2
        + [dma((levels, 4, HALVES, 3))] * 2
        + [dma((levels, 2, 3))] * 2
        + [dma((4,))] * 2,
        compiler_params=pltpu.CompilerParams(
            collective_id=0, has_side_effects=True, vmem_limit_bytes=56 * 1024 * 1024
        ),
        cost_estimate=pl.CostEstimate(
            flops=2 * harm**3 * 60, bytes_accessed=2**20, transcendentals=0
        ),
    )(mode_matrix, aux)
    return result[None]


def solution(mesh):
    n, nb = mesh.shape["layer"], mesh.shape["blk"]
    placed = (P(None, "layer", "blk"), P(None, "layer"), P(None, "layer"))
    return jax.shard_map(
        functools.partial(on_device, n, nb),
        mesh=mesh,
        in_specs=placed,
        out_specs=P("layer", None, "blk", None),
        check_vma=False,
    )
```

```python
import functools

import jax
import jax.numpy as jnp
from jax import lax
from jax.experimental import pallas as pl
from jax.experimental.pallas import tpu as pltpu
from jax.sharding import PartitionSpec as P

REFL = 4
LANES = 128
HALVES = 2
MESH = pl.DeviceIdType.MESH


def dot(left_op, right_op):
    return jnp.dot(left_op, right_op, preferred_element_type=jnp.float32)


def stack_kernel(
    n, nb, levels,
    mode_ref, aux_ref, out_ref,
    mrecv, arecv, modes, scaled, layer_s, state, land,
    down, up, left, right, mid,
    mode_send, mode_recv, aux_send, aux_recv, share_send, share_recv,
    far_send, far_recv, relay_send, relay_recv, join_send, join_recv,
):
    group = lax.axis_index("layer")
    blk = lax.axis_index("blk")
    cross = lax.rem(blk + 2, nb)
    sib = blk + 1 - 2 * lax.rem(blk, 2)
    sib_cross = lax.rem(sib + 2, nb)
    harm = state.shape[-1]
    rows = harm // nb
    lay = mode_ref.shape[0] // n
    mode_local = harm // n

    def cut(index):
        return slice(index * rows, (index + 1) * rows)

    own = pl.ds(pl.multiple_of(blk * rows, rows), rows)

    barrier = pltpu.get_barrier_semaphore()

    def greet(offset, carry):
        pl.semaphore_signal(
            barrier, inc=1, device_id=(lax.rem(group + offset, n), blk), device_id_type=MESH
        )
        return carry

    lax.fori_loop(1, n, greet, 0)
    for other in (cross, sib):
        pl.semaphore_signal(barrier, inc=1, device_id=(group, other), device_id_type=MESH)
    pl.semaphore_wait(barrier, n + 1)

    def mode_copy(offset, layer):
        target = lax.rem(group + offset, n)
        return pltpu.make_async_remote_copy(
            src_ref=mode_ref.at[target * lay + layer],
            dst_ref=mrecv.at[blk, layer, group],
            send_sem=mode_send.at[offset, layer],
            recv_sem=mode_recv.at[offset, layer],
            device_id=(target, blk),
            device_id_type=MESH,
        )

    def aux_copy(offset):
        target = lax.rem(group + offset, n)
        return pltpu.make_async_remote_copy(
            src_ref=aux_ref.at[target],
            dst_ref=arecv.at[group],
            send_sem=aux_send.at[offset],
            recv_sem=aux_recv.at[offset],
            device_id=(target, blk),
            device_id_type=MESH,
        )

    def for_offsets(body):
        def step(offset, carry):
            body(offset)
            return carry

        lax.fori_loop(1, n, step, 0)

    for layer in range(lay):
        for_offsets(lambda offset: mode_copy(offset, layer).start())
        if layer == 0:
            for_offsets(lambda offset: aux_copy(offset).start())
        mrecv[blk, layer, group] = mode_ref[group * lay + layer]
    arecv[group] = aux_ref[group]

    def share_copy(layer, offset, index, piece, other):
        where = mrecv.at[piece, layer, lax.rem(group + n - offset, n)]
        return pltpu.make_async_remote_copy(
            src_ref=where,
            dst_ref=where,
            send_sem=share_send.at[layer, offset, index],
            recv_sem=share_recv.at[layer, offset, index],
            device_id=(group, other),
            device_id_type=MESH,
        )

    def share_first(layer, offset):
        share_copy(layer, offset, 0, blk, cross).start()
        share_copy(layer, offset, 1, blk, sib).start()

    def share_second(layer):
        def step(offset, carry):
            share_copy(layer, offset, 0, cross, cross).wait_recv()
            share_copy(layer, offset, 2, cross, sib).start()
            return carry

        lax.fori_loop(0, n, step, 0)

    def share_end(layer):
        def step(offset, carry):
            share_copy(layer, offset, 1, sib, sib).wait_recv()
            share_copy(layer, offset, 2, sib_cross, sib).wait_recv()
            return carry

        lax.fori_loop(0, n, step, 0)

    def share_left(layer):
        def step(offset, carry):
            share_copy(layer, offset, 0, blk, cross).wait_send()
            share_copy(layer, offset, 1, blk, sib).wait_send()
            share_copy(layer, offset, 2, cross, sib).wait_send()
            return carry

        lax.fori_loop(0, n, step, 0)

    for layer in range(lay):
        share_first(layer, 0)
    for layer in range(lay):
        def pass_on(offset, layer=layer):
            mode_copy(offset, layer).wait_recv()
            share_first(layer, offset)

        for_offsets(pass_on)
    for_offsets(lambda offset: aux_copy(offset).wait_recv())
    per_window = LANES // mode_local
    windows = [
        sum(arecv[index] for index in range(w * per_window, (w + 1) * per_window))
        for w in range(harm // LANES)
    ]

    share_second(0)
    for layer in range(lay):
        share_end(layer)
        if layer + 1 < lay:
            share_second(layer + 1)
        for piece in range(nb):
            cols = cut(piece)
            wide = mrecv[piece, layer].astype(jnp.float32).reshape(harm, rows)
            coeff = windows[piece]
            modes[:, cols] = wide.astype(jnp.bfloat16)
            scaled[0, :, cols] = (wide * coeff[lay + layer][None]).astype(jnp.bfloat16)
            scaled[1, :, cols] = (wide * coeff[layer][None]).astype(jnp.bfloat16)
        for kind in range(2):
            layer_s[layer, kind] = lax.dot_general(
                modes[...], scaled[kind], (((1,), (1,)), ((), ())),
                preferred_element_type=jnp.float32,
            ).astype(jnp.bfloat16)
        layer_s[layer, 2] = -layer_s[layer, 0]

    def piece_rows(quarter, half):
        size = rows // HALVES
        return pl.ds(pl.multiple_of(quarter * rows + half * size, size), size)

    def far_copy(level, distance, slot, part, half):
        return pltpu.make_async_remote_copy(
            src_ref=state.at[slot, part, piece_rows(blk, half)],
            dst_ref=land.at[level, part, piece_rows(blk, half)],
            send_sem=far_send.at[level, part, half],
            recv_sem=far_recv.at[level, part, half],
            device_id=(lax.rem(group + distance, n), blk),
            device_id_type=MESH,
        )

    def send_far(level, distance, slot, part):
        @pl.when(group + distance < n)
        def _():
            for half in range(HALVES):
                far_copy(level, distance, slot, part, half).start()

    def far_left(level):
        for part in range(4):
            for half in range(HALVES):
                far_copy(level, 1, 0, part, half).wait_send()

    def join_copy(slot, part, index, quarter, other):
        where = state.at[slot, part, pl.ds(pl.multiple_of(quarter * rows, rows), rows)]
        return pltpu.make_async_remote_copy(
            src_ref=where,
            dst_ref=where,
            send_sem=join_send.at[slot, part, index],
            recv_sem=join_recv.at[slot, part, index],
            device_id=(group, other),
            device_id_type=MESH,
        )

    def join_first(slot, part):
        join_copy(slot, part, 0, blk, cross).start()
        join_copy(slot, part, 1, blk, sib).start()

    def join_second(slot):
        for part in (1, 0):
            join_copy(slot, part, 0, cross, cross).wait_recv()
            join_copy(slot, part, 2, cross, sib).start()

    def join_end(slot):
        for part in (1, 0):
            join_copy(slot, part, 1, sib, sib).wait_recv()
            join_copy(slot, part, 2, sib_cross, sib).wait_recv()

    def relay_copy(level, part, half, index, piece, other):
        where = land.at[level, part, piece_rows(piece, half)]
        return pltpu.make_async_remote_copy(
            src_ref=where,
            dst_ref=where,
            send_sem=relay_send.at[level, part, half, index],
            recv_sem=relay_recv.at[level, part, half, index],
            device_id=(group, other),
            device_id_type=MESH,
        )

    def relay_first(level, part):
        for half in range(HALVES):
            far_copy(level, 1, 0, part, half).wait_recv()
            if part >= 2:
                relay_copy(level, part, half, 0, blk, cross).start()
                relay_copy(level, part, half, 1, blk, sib).start()

    def relay_second(level, part):
        for half in range(HALVES):
            relay_copy(level, part, half, 0, cross, cross).wait_recv()
            relay_copy(level, part, half, 2, cross, sib).start()

    def relay_end(level, part):
        for half in range(HALVES):
            relay_copy(level, part, half, 1, sib, sib).wait_recv()
            relay_copy(level, part, half, 2, sib_cross, sib).wait_recv()

    def chain(total, start, coupling, repeat):
        source = start if repeat == 0 else total
        total[...] = (start[...] + dot(source[...], coupling[...])).astype(jnp.bfloat16)

    def own_star(upper, lower, put, first, second, end, join, ahead):
        a11, a12, a21, a22 = upper
        b11, b12, b21, b22 = lower
        a11, a12, b21, b22 = [ref.at[own] for ref in (a11, a12, b21, b22)]
        first(3)
        join(0)
        second(3)
        join(1)
        end(3)
        up[...] = dot(a22[...], b11[...]).astype(jnp.bfloat16)
        chain(right, b21, up, 0)
        first(2)
        for repeat in range(1, REFL):
            chain(right, b21, up, repeat)
        mid[...] = dot(right[...], a22[...]).astype(jnp.bfloat16)
        put(3, b22[...] + dot(mid[...], b12[...]))
        second(2)
        down[...] = dot(b11[...], a22[...]).astype(jnp.bfloat16)
        end(2)
        put(2, dot(right[...], a21[...]))
        first(1)
        ahead(0)
        for repeat in range(REFL):
            chain(left, a12, down, repeat)
        put(1, dot(left[...], b12[...]))
        mid[...] = dot(left[...], b11[...]).astype(jnp.bfloat16)
        first(0)
        put(0, a11[...] + dot(mid[...], a21[...]))
        ahead(1)

    def parts(ref):
        return [ref.at[part] for part in range(4)]

    def layer_parts(layer):
        refl, tran, back = [layer_s.at[layer, kind] for kind in range(3)]
        return [refl, tran, tran, back]

    def nothing(*where):
        pass

    last = levels - 1
    assert lay == 2 and nb == 4 and last >= 1
    def put_state(level, distance):
        def put(part, value):
            state[level, part, own] = value.astype(jnp.bfloat16)
            send_far(level, distance, level, part)
            if part < 2:
                join_first(level, part)

        return put

    own_star(
        layer_parts(0), layer_parts(1), put_state(0, 1), nothing, nothing, nothing, nothing,
        nothing,
    )

    slot_end = sum(jnp.where(group >= (1 << k), 1, 0) for k in range(last))
    half = 1 << last
    middle = jnp.logical_and(group >= half, 2 * group < 3 * half)
    not_middle = jnp.logical_not(middle)

    def relay_ahead(step):
        for part in (3, 2):
            (relay_first, relay_second)[step](last, part)

    def one_level(level, distance):
        @pl.when(group >= distance)
        def _():
            own_star(
                parts(land.at[level]), parts(state.at[level]), put_state(level + 1, 2 * distance),
                functools.partial(relay_first, level),
                functools.partial(relay_second, level),
                functools.partial(relay_end, level),
                lambda step: (join_second, join_end)[step](level),
                lambda step: pl.when(jnp.logical_and(level == last - 1, middle))(
                    lambda: relay_ahead(step)
                ),
            )

        @pl.when(group < distance)
        def _():
            @pl.when(jnp.logical_or(level == 0, 2 * group >= distance))
            def _():
                join_second(level)
                join_end(level)

            far_left(level)

            @pl.when(level == last - 2)
            def _():
                for part in (3, 2):
                    send_far(last, half, slot_end, part)

            for part in (3, 2):
                @pl.when(jnp.logical_or(level < last - 1, 4 * group >= half))
                def _(part=part):
                    send_far(level + 1, 2 * distance, slot_end, part)
            for part in (1, 0):
                send_far(level + 1, 2 * distance, slot_end, part)

        return 2 * distance

    lax.fori_loop(0, last, one_level, 1)

    @pl.when(group < half)
    def _():
        @pl.when(2 * group >= half)
        def _():
            join_second(last)
            join_end(last)

        out_ref[...] = -state[slot_end, :, own]

    def put_out(part, value):
        out_ref[part] = -value.astype(jnp.bfloat16)

    def last_first(part):
        if part >= 2:
            pl.when(not_middle)(lambda: relay_first(last, part))
        else:
            relay_first(last, part)

    @pl.when(group >= half)
    def _():
        own_star(
            parts(land.at[last]), parts(state.at[last]), put_out,
            last_first,
            lambda part: pl.when(not_middle)(lambda: relay_second(last, part)),
            functools.partial(relay_end, last),
            lambda step: (join_second, join_end)[step](last),
            nothing,
        )

    for layer in range(lay):
        for_offsets(lambda offset: mode_copy(offset, layer).wait_send())
        share_left(layer)
    for_offsets(lambda offset: aux_copy(offset).wait_send())
    for level in range(levels):
        reach = 1 << level
        sends = group + reach < n
        if level < last:
            sends = jnp.logical_and(sends, group >= reach)

        @pl.when(sends)
        def _(level=level):
            far_left(level)

        @pl.when(group >= reach)
        def _(level=level):
            for part in (2, 3):
                for piece in range(HALVES):
                    relay_copy(level, part, piece, 0, blk, cross).wait_send()
                    relay_copy(level, part, piece, 1, blk, sib).wait_send()
                    relay_copy(level, part, piece, 2, cross, sib).wait_send()

        @pl.when(2 * group >= reach if level else group >= 0)
        def _(level=level):
            for part in range(2):
                join_copy(level, part, 0, blk, cross).wait_send()
                join_copy(level, part, 1, blk, sib).wait_send()
                join_copy(level, part, 2, cross, sib).wait_send()


def on_device(n, nb, mode_matrix, decay_rate, facet_refl):
    layers, mode_local = decay_rate.shape
    harm = n * mode_matrix.shape[1]
    lay = layers // n
    levels = n.bit_length() - 1
    refl = facet_refl.astype(jnp.float32)
    tran = jnp.sqrt(1.0 - refl * refl) * jnp.exp(-decay_rate.astype(jnp.float32))
    coeff = jnp.concatenate(
        [tran.reshape(n, lay, mode_local), refl.reshape(n, lay, mode_local)], axis=1
    )
    coeff = jnp.pad(coeff, ((0, 0), (0, 8 - 2 * lay), (0, 0)))
    copies = LANES // mode_local
    place = lax.broadcasted_iota(jnp.int32, (1, 1, LANES), 2) // mode_local
    aux = jnp.where(
        place == lax.rem(lax.axis_index("layer"), copies), jnp.tile(coeff, (1, 1, copies)), 0.0
    )
    square = (harm, harm)
    dma = pltpu.SemaphoreType.DMA
    vmem = pl.BlockSpec(memory_space=pltpu.VMEM)
    result = pl.pallas_call(
        functools.partial(stack_kernel, n, nb, levels),
        out_shape=jax.ShapeDtypeStruct((4, harm // nb, harm), jnp.bfloat16),
        in_specs=[vmem, vmem],
        out_specs=vmem,
        scratch_shapes=[
            pltpu.VMEM((nb, lay, n) + mode_matrix.shape[1:], jnp.bfloat16),
            pltpu.VMEM((n, 8, LANES), jnp.float32),
            pltpu.VMEM(square, jnp.bfloat16),
            pltpu.VMEM((2,) + square, jnp.bfloat16),
            pltpu.VMEM((lay, 3) + square, jnp.bfloat16),
            pltpu.VMEM((levels, 4) + square, jnp.bfloat16),
            pltpu.VMEM((levels, 4) + square, jnp.bfloat16),
        ]
        + [pltpu.VMEM(square, jnp.bfloat16)] * 2
        + [pltpu.VMEM((harm // nb, harm), jnp.bfloat16)] * 3
        + [dma((n, lay))] * 2
        + [dma((n,))] * 2
        + [dma((lay, n, 3))] * 2
        + [dma((levels, 4, HALVES))] * 2
        + [dma((levels, 4, HALVES, 3))] * 2
        + [dma((levels, 2, 3))] * 2,
        compiler_params=pltpu.CompilerParams(
            collective_id=0, has_side_effects=True, vmem_limit_bytes=56 * 1024 * 1024
        ),
        cost_estimate=pl.CostEstimate(
            flops=2 * harm**3 * 60, bytes_accessed=2**20, transcendentals=0
        ),
    )(mode_matrix, aux)
    return -result[None]


def solution(mesh):
    n, nb = mesh.shape["layer"], mesh.shape["blk"]
    placed = (P(None, "layer", "blk"), P(None, "layer"), P(None, "layer"))
    return jax.shard_map(
        functools.partial(on_device, n, nb),
        mesh=mesh,
        in_specs=placed,
        out_specs=P("layer", None, "blk", None),
        check_vma=False,
    )
```

```python
import functools

import jax
import jax.numpy as jnp
from jax import lax
from jax.experimental import pallas as pl
from jax.experimental.pallas import tpu as pltpu
from jax.sharding import PartitionSpec as P

REFL = 4
LANES = 128
HALVES = 2
MESH = pl.DeviceIdType.MESH


def dot(left_op, right_op):
    return jnp.dot(left_op, right_op, preferred_element_type=jnp.float32)


def stack_kernel(
    n, nb, levels,
    mode_ref, aux_ref, out_ref,
    mrecv, arecv, modes, scaled, layer_s, state, land,
    up, total, mid,
    mode_send, mode_recv, aux_send, aux_recv, share_send, share_recv,
    far_send, far_recv, relay_send, relay_recv, join_send, join_recv,
    swap_send, swap_recv,
):
    group = lax.axis_index("layer")
    blk = lax.axis_index("blk")
    cross = lax.rem(blk + 2, nb)
    sib = blk + 1 - 2 * lax.rem(blk, 2)
    sib_cross = lax.rem(sib + 2, nb)
    harm = state.shape[-1]
    rows = harm // nb
    lay = mode_ref.shape[0] // n
    mode_local = harm // n

    def cut(index):
        return slice(index * rows, (index + 1) * rows)

    role = lax.rem(blk, 2)
    lead_part, next_part = 3 - 2 * role, 2 - 2 * role
    own = pl.ds(pl.multiple_of(blk * rows, rows), rows)
    sib_own = pl.ds(pl.multiple_of(sib * rows, rows), rows)
    wing = 2 * rows

    def wing_of(device):
        return pl.ds(pl.multiple_of(lax.div(device, 2) * wing, wing), wing)

    mine = wing_of(blk)

    barrier = pltpu.get_barrier_semaphore()

    def greet(offset, carry):
        pl.semaphore_signal(
            barrier, inc=1, device_id=(lax.rem(group + offset, n), blk), device_id_type=MESH
        )
        return carry

    lax.fori_loop(1, n, greet, 0)
    for other in (cross, sib):
        pl.semaphore_signal(barrier, inc=1, device_id=(group, other), device_id_type=MESH)
    pl.semaphore_wait(barrier, n + 1)

    def mode_copy(offset, layer):
        target = lax.rem(group + offset, n)
        return pltpu.make_async_remote_copy(
            src_ref=mode_ref.at[target * lay + layer],
            dst_ref=mrecv.at[blk, layer, group],
            send_sem=mode_send.at[offset, layer],
            recv_sem=mode_recv.at[offset, layer],
            device_id=(target, blk),
            device_id_type=MESH,
        )

    def aux_copy(offset):
        target = lax.rem(group + offset, n)
        return pltpu.make_async_remote_copy(
            src_ref=aux_ref.at[target],
            dst_ref=arecv.at[group],
            send_sem=aux_send.at[offset],
            recv_sem=aux_recv.at[offset],
            device_id=(target, blk),
            device_id_type=MESH,
        )

    def for_offsets(body):
        def step(offset, carry):
            body(offset)
            return carry

        lax.fori_loop(1, n, step, 0)

    for layer in range(lay):
        for_offsets(lambda offset: mode_copy(offset, layer).start())
        if layer == 0:
            for_offsets(lambda offset: aux_copy(offset).start())
        mrecv[blk, layer, group] = mode_ref[group * lay + layer]
    arecv[group] = aux_ref[group]

    def share_copy(layer, offset, index, piece, other):
        where = mrecv.at[piece, layer, lax.rem(group + n - offset, n)]
        return pltpu.make_async_remote_copy(
            src_ref=where,
            dst_ref=where,
            send_sem=share_send.at[layer, offset, index],
            recv_sem=share_recv.at[layer, offset, index],
            device_id=(group, other),
            device_id_type=MESH,
        )

    def share_first(layer, offset):
        share_copy(layer, offset, 0, blk, cross).start()
        share_copy(layer, offset, 1, blk, sib).start()

    def share_second(layer):
        def step(offset, carry):
            share_copy(layer, offset, 0, cross, cross).wait_recv()
            share_copy(layer, offset, 2, cross, sib).start()
            return carry

        lax.fori_loop(0, n, step, 0)

    def share_end(layer):
        def step(offset, carry):
            share_copy(layer, offset, 1, sib, sib).wait_recv()
            share_copy(layer, offset, 2, sib_cross, sib).wait_recv()
            return carry

        lax.fori_loop(0, n, step, 0)

    def share_left(layer):
        def step(offset, carry):
            share_copy(layer, offset, 0, blk, cross).wait_send()
            share_copy(layer, offset, 1, blk, sib).wait_send()
            share_copy(layer, offset, 2, cross, sib).wait_send()
            return carry

        lax.fori_loop(0, n, step, 0)

    for layer in range(lay):
        share_first(layer, 0)
    for layer in range(lay):
        def pass_on(offset, layer=layer):
            mode_copy(offset, layer).wait_recv()
            share_first(layer, offset)

        for_offsets(pass_on)
    for_offsets(lambda offset: aux_copy(offset).wait_recv())
    per_window = LANES // mode_local
    windows = [
        sum(arecv[index] for index in range(w * per_window, (w + 1) * per_window))
        for w in range(harm // LANES)
    ]

    share_second(0)
    for layer in range(lay):
        share_end(layer)
        if layer + 1 < lay:
            share_second(layer + 1)
        for piece in range(nb):
            cols = cut(piece)
            wide = mrecv[piece, layer].astype(jnp.float32).reshape(harm, rows)
            coeff = windows[piece]
            modes[:, cols] = wide.astype(jnp.bfloat16)
            scaled[0, :, cols] = (wide * coeff[lay + layer][None]).astype(jnp.bfloat16)
            scaled[1, :, cols] = (wide * coeff[layer][None]).astype(jnp.bfloat16)
        for kind in range(2):
            layer_s[layer, kind] = lax.dot_general(
                modes[...], scaled[kind], (((1,), (1,)), ((), ())),
                preferred_element_type=jnp.float32,
            ).astype(jnp.bfloat16)
        layer_s[layer, 2] = -layer_s[layer, 0]

    def piece_rows(device, half):
        size = wing // HALVES
        return pl.ds(pl.multiple_of(lax.div(device, 2) * wing + half * size, size), size)

    def far_copy(level, distance, slot, part, half):
        return pltpu.make_async_remote_copy(
            src_ref=state.at[slot, part, piece_rows(blk, half)],
            dst_ref=land.at[level, part, piece_rows(blk, half)],
            send_sem=far_send.at[level, part, half],
            recv_sem=far_recv.at[level, part, half],
            device_id=(lax.rem(group + distance, n), blk),
            device_id_type=MESH,
        )

    def send_far(level, distance, slot, part):
        @pl.when(group + distance < n)
        def _():
            for half in range(HALVES):
                far_copy(level, distance, slot, part, half).start()

    def far_left(level):
        for part in (lead_part, next_part):
            for half in range(HALVES):
                far_copy(level, 1, 0, part, half).wait_send()

    def far_end(level, part):
        for half in range(HALVES):
            far_copy(level, 1, 0, part, half).wait_recv()

    def join_copy(slot, part):
        return pltpu.make_async_remote_copy(
            src_ref=state.at[slot, part],
            dst_ref=state.at[slot, part],
            send_sem=join_send.at[slot, part],
            recv_sem=join_recv.at[slot, part],
            device_id=(group, sib),
            device_id_type=MESH,
        )

    def join_end(slot):
        for part in (1, 0):
            join_copy(slot, part).wait_recv()

    def join(slot):
        pl.when(role == 0)(lambda: join_end(slot))

    def relay_copy(level, part, half, index, device, other):
        where = land.at[level, part, piece_rows(device, half)]
        return pltpu.make_async_remote_copy(
            src_ref=where,
            dst_ref=where,
            send_sem=relay_send.at[level, part, half, index],
            recv_sem=relay_recv.at[level, part, half, index],
            device_id=(group, other),
            device_id_type=MESH,
        )

    def relay_first(level, part):
        for half in range(HALVES):
            far_copy(level, 1, 0, part, half).wait_recv()
            relay_copy(level, part, half, 0, blk, cross).start()
            relay_copy(level, part, half, 1, blk, sib).start()

    def near_first(level, part):
        for half in range(HALVES):
            far_copy(level, 1, 0, part, half).wait_recv()
            relay_copy(level, part, half, 0, blk, cross).start()

    def near_end(level, part):
        for half in range(HALVES):
            relay_copy(level, part, half, 0, cross, cross).wait_recv()

    def relay_second(level, part):
        for half in range(HALVES):
            relay_copy(level, part, half, 0, cross, cross).wait_recv()
            relay_copy(level, part, half, 2, cross, sib).start()

    def relay_end(level, part):
        for half in range(HALVES):
            relay_copy(level, part, half, 1, sib, sib).wait_recv()
            relay_copy(level, part, half, 2, sib_cross, sib).wait_recv()

    def swap_copy(slot, part):
        return pltpu.make_async_remote_copy(
            src_ref=state.at[slot, part, sib_own],
            dst_ref=out_ref.at[part],
            send_sem=swap_send.at[part],
            recv_sem=swap_recv.at[part],
            device_id=(group, sib),
            device_id_type=MESH,
        )

    def put_out(slot, part):
        swap_copy(slot, part).start()
        out_ref[part] = state[slot, part, own]

    def chain(total, start, coupling, repeat):
        source = start if repeat == 0 else total
        total[...] = (start[...] + dot(source[...], coupling[...])).astype(jnp.bfloat16)

    def under_star(upper, lower, put, level, rows_now, final):
        a11, a12, a21, a22 = upper
        b11, b12, b21, b22 = lower
        b21, b22 = b21.at[rows_now], b22.at[rows_now]
        acc, part_mid = total.at[: b21.shape[0]], mid.at[: b21.shape[0]]
        if level is not None:
            relay_first(level, 3)
            join_end(level)
            relay_second(level, 3)
        up[...] = dot(a22[...], b11[...]).astype(jnp.bfloat16)
        chain(acc, b21, up, 0)
        chain(acc, b21, up, 1)
        if level is not None:
            relay_first(level, 2)
        chain(acc, b21, up, 2)
        chain(acc, b21, up, 3)
        part_mid[...] = dot(acc[...], a22[...]).astype(jnp.bfloat16)
        put(3, b22[...] + dot(part_mid[...], b12[...]))
        if level is not None:
            relay_second(level, 2)
        put(2, dot(acc[...], a21[...]))

    def over_star(upper, lower, put, level, rows_now, final):
        a11, a12, a21, a22 = upper
        b11, b12, b21, b22 = lower
        a11, a12 = a11.at[rows_now], a12.at[rows_now]
        acc, part_mid = total.at[: a11.shape[0]], mid.at[: a11.shape[0]]
        if level is not None:
            relay_end(level, 3)
        up[...] = dot(b11[...], a22[...]).astype(jnp.bfloat16)
        if level is not None:
            if final:
                far_end(level, 1)
            else:
                near_first(level, 1)
                near_end(level, 1)
        chain(acc, a12, up, 0)
        chain(acc, a12, up, 1)
        if level is not None and not final:
            near_first(level, 0)
        chain(acc, a12, up, 2)
        chain(acc, a12, up, 3)
        put(1, dot(acc[...], b12[...]))
        part_mid[...] = dot(acc[...], b11[...]).astype(jnp.bfloat16)
        if level is not None:
            if final:
                far_end(level, 0)
            else:
                near_end(level, 0)
            relay_end(level, 2)
        put(0, a11[...] + dot(part_mid[...], a21[...]))

    def star(upper, lower, put, level, rows_now=slice(None), final=False):
        for own_role, form in enumerate((under_star, over_star)):
            pl.when(role == own_role)(
                functools.partial(form, upper, lower, put, level, rows_now, final)
            )

    def parts(ref):
        return [ref.at[part] for part in range(4)]

    def layer_parts(layer):
        refl, tran, back = [layer_s.at[layer, kind] for kind in range(3)]
        return [refl, tran, tran, back]

    last = levels - 1
    assert lay == 2 and nb == 4 and last >= 1

    def put_state(level, distance):
        def put(part, value):
            state[level, part] = value.astype(jnp.bfloat16)
            send_far(level, distance, level, part)
            if part < 2:
                join_copy(level, part).start()

        return put

    star(layer_parts(0), layer_parts(1), put_state(0, 1), None)

    slot_end = sum(jnp.where(group >= (1 << k), 1, 0) for k in range(last))
    half = 1 << last

    def one_level(level, distance):
        @pl.when(group >= distance)
        def _():
            star(
                parts(land.at[level]), parts(state.at[level]),
                put_state(level + 1, 2 * distance), level,
            )

        @pl.when(group < distance)
        def _():
            @pl.when(jnp.logical_or(level == 0, 2 * group >= distance))
            def _():
                join(level)

            far_left(level)

            @pl.when(level == last - 2)
            def _():
                send_far(last, half, slot_end, lead_part)

            @pl.when(jnp.logical_or(level < last - 1, 4 * group >= half))
            def _():
                send_far(level + 1, 2 * distance, slot_end, lead_part)

            send_far(level + 1, 2 * distance, slot_end, next_part)

        return 2 * distance

    lax.fori_loop(0, last, one_level, 1)

    @pl.when(group < half)
    def _():
        @pl.when(2 * group >= half)
        def _():
            join(last)

        put_out(slot_end, lead_part)
        put_out(slot_end, next_part)

    def put_last(part, value):
        state[levels, part, mine] = value.astype(jnp.bfloat16)
        put_out(levels, part)

    @pl.when(group >= half)
    def _():
        star(parts(land.at[last]), parts(state.at[last]), put_last, last, mine, True)

    for part in (3 - lead_part, 3 - next_part):
        swap_copy(0, part).wait_recv()

    for layer in range(lay):
        for_offsets(lambda offset: mode_copy(offset, layer).wait_send())
        share_left(layer)
    for_offsets(lambda offset: aux_copy(offset).wait_send())
    for level in range(levels):
        reach = 1 << level
        sends = group + reach < n
        if level < last:
            sends = jnp.logical_and(sends, group >= reach)

        @pl.when(sends)
        def _(level=level):
            far_left(level)

        @pl.when(jnp.logical_and(group >= reach, role == 0))
        def _(level=level):
            for part in (2, 3):
                for piece in range(HALVES):
                    relay_copy(level, part, piece, 0, blk, cross).wait_send()
                    relay_copy(level, part, piece, 1, blk, sib).wait_send()
                    relay_copy(level, part, piece, 2, cross, sib).wait_send()

        if level < last:
            @pl.when(jnp.logical_and(group >= reach, role == 1))
            def _(level=level):
                for part in range(2):
                    for piece in range(HALVES):
                        relay_copy(level, part, piece, 0, blk, cross).wait_send()

        formed = 2 * group >= reach if level else group >= 0

        @pl.when(jnp.logical_and(formed, role == 1))
        def _(level=level):
            for part in range(2):
                join_copy(level, part).wait_send()

    for part in (lead_part, next_part):
        swap_copy(0, part).wait_send()


def on_device(n, nb, mode_matrix, decay_rate, facet_refl):
    layers, mode_local = decay_rate.shape
    harm = n * mode_matrix.shape[1]
    lay = layers // n
    levels = n.bit_length() - 1
    refl = facet_refl.astype(jnp.float32)
    tran = jnp.sqrt(1.0 - refl * refl) * jnp.exp(-decay_rate.astype(jnp.float32))
    coeff = jnp.concatenate(
        [tran.reshape(n, lay, mode_local), refl.reshape(n, lay, mode_local)], axis=1
    )
    coeff = jnp.pad(coeff, ((0, 0), (0, 8 - 2 * lay), (0, 0)))
    copies = LANES // mode_local
    place = lax.broadcasted_iota(jnp.int32, (1, 1, LANES), 2) // mode_local
    aux = jnp.where(
        place == lax.rem(lax.axis_index("layer"), copies), jnp.tile(coeff, (1, 1, copies)), 0.0
    )
    square = (harm, harm)
    dma = pltpu.SemaphoreType.DMA
    vmem = pl.BlockSpec(memory_space=pltpu.VMEM)
    result = pl.pallas_call(
        functools.partial(stack_kernel, n, nb, levels),
        out_shape=jax.ShapeDtypeStruct((4, harm // nb, harm), jnp.bfloat16),
        in_specs=[vmem, vmem],
        out_specs=vmem,
        scratch_shapes=[
            pltpu.VMEM((nb, lay, n) + mode_matrix.shape[1:], jnp.bfloat16),
            pltpu.VMEM((n, 8, LANES), jnp.float32),
            pltpu.VMEM(square, jnp.bfloat16),
            pltpu.VMEM((2,) + square, jnp.bfloat16),
            pltpu.VMEM((lay, 3) + square, jnp.bfloat16),
            pltpu.VMEM((levels + 1, 4) + square, jnp.bfloat16),
            pltpu.VMEM((levels, 4) + square, jnp.bfloat16),
        ]
        + [pltpu.VMEM(square, jnp.bfloat16)] * 3
        + [dma((n, lay))] * 2
        + [dma((n,))] * 2
        + [dma((lay, n, 3))] * 2
        + [dma((levels, 4, HALVES))] * 2
        + [dma((levels, 4, HALVES, 3))] * 2
        + [dma((levels, 2))] * 2
        + [dma((4,))] * 2,
        compiler_params=pltpu.CompilerParams(
            collective_id=0, has_side_effects=True, vmem_limit_bytes=56 * 1024 * 1024
        ),
        cost_estimate=pl.CostEstimate(
            flops=2 * harm**3 * 60, bytes_accessed=2**20, transcendentals=0
        ),
    )(mode_matrix, aux)
    return result[None]


def solution(mesh):
    n, nb = mesh.shape["layer"], mesh.shape["blk"]
    placed = (P(None, "layer", "blk"), P(None, "layer"), P(None, "layer"))
    return jax.shard_map(
        functools.partial(on_device, n, nb),
        mesh=mesh,
        in_specs=placed,
        out_specs=P("layer", None, "blk", None),
        check_vma=False,
    )
```

```python
import functools

import jax
import jax.numpy as jnp
from jax import lax
from jax.experimental import pallas as pl
from jax.experimental.pallas import tpu as pltpu
from jax.sharding import PartitionSpec as P

REFL = 4
LANES = 128
HALVES = 1
MESH = pl.DeviceIdType.MESH


def dot(left_op, right_op):
    return jnp.dot(left_op, right_op, preferred_element_type=jnp.float32)


def stack_kernel(
    n, nb, levels,
    mode_ref, aux_ref, out_ref,
    mrecv, arecv, modes, scaled, layer_s, state, land,
    down, up, left, right, mid,
    mode_send, mode_recv, aux_send, aux_recv, share_send, share_recv,
    far_send, far_recv, relay_send, relay_recv, join_send, join_recv,
):
    group = lax.axis_index("layer")
    blk = lax.axis_index("blk")
    cross = lax.rem(blk + 2, nb)
    sib = blk + 1 - 2 * lax.rem(blk, 2)
    sib_cross = lax.rem(sib + 2, nb)
    harm = state.shape[-1]
    rows = harm // nb
    lay = mode_ref.shape[0] // n
    mode_local = harm // n

    def cut(index):
        return slice(index * rows, (index + 1) * rows)

    own = pl.ds(pl.multiple_of(blk * rows, rows), rows)

    barrier = pltpu.get_barrier_semaphore()

    def greet(offset, carry):
        pl.semaphore_signal(
            barrier, inc=1, device_id=(lax.rem(group + offset, n), blk), device_id_type=MESH
        )
        return carry

    lax.fori_loop(1, n, greet, 0)
    for other in (cross, sib):
        pl.semaphore_signal(barrier, inc=1, device_id=(group, other), device_id_type=MESH)
    pl.semaphore_wait(barrier, n + 1)

    def mode_copy(offset, layer):
        target = lax.rem(group + offset, n)
        return pltpu.make_async_remote_copy(
            src_ref=mode_ref.at[target * lay + layer],
            dst_ref=mrecv.at[blk, layer, group],
            send_sem=mode_send.at[offset, layer],
            recv_sem=mode_recv.at[offset, layer],
            device_id=(target, blk),
            device_id_type=MESH,
        )

    def aux_copy(offset):
        target = lax.rem(group + offset, n)
        return pltpu.make_async_remote_copy(
            src_ref=aux_ref.at[target],
            dst_ref=arecv.at[group],
            send_sem=aux_send.at[offset],
            recv_sem=aux_recv.at[offset],
            device_id=(target, blk),
            device_id_type=MESH,
        )

    def for_offsets(body):
        def step(offset, carry):
            body(offset)
            return carry

        lax.fori_loop(1, n, step, 0)

    for layer in range(lay):
        for_offsets(lambda offset: mode_copy(offset, layer).start())
        if layer == 0:
            for_offsets(lambda offset: aux_copy(offset).start())
        mrecv[blk, layer, group] = mode_ref[group * lay + layer]
    arecv[group] = aux_ref[group]

    def share_copy(layer, offset, index, piece, other):
        where = mrecv.at[piece, layer, lax.rem(group + n - offset, n)]
        return pltpu.make_async_remote_copy(
            src_ref=where,
            dst_ref=where,
            send_sem=share_send.at[layer, offset, index],
            recv_sem=share_recv.at[layer, offset, index],
            device_id=(group, other),
            device_id_type=MESH,
        )

    def share_first(layer, offset):
        share_copy(layer, offset, 0, blk, cross).start()
        share_copy(layer, offset, 1, blk, sib).start()

    def share_second(layer):
        def step(offset, carry):
            share_copy(layer, offset, 0, cross, cross).wait_recv()
            share_copy(layer, offset, 2, cross, sib).start()
            return carry

        lax.fori_loop(0, n, step, 0)

    def share_end(layer):
        def step(offset, carry):
            share_copy(layer, offset, 1, sib, sib).wait_recv()
            share_copy(layer, offset, 2, sib_cross, sib).wait_recv()
            return carry

        lax.fori_loop(0, n, step, 0)

    def share_left(layer):
        def step(offset, carry):
            share_copy(layer, offset, 0, blk, cross).wait_send()
            share_copy(layer, offset, 1, blk, sib).wait_send()
            share_copy(layer, offset, 2, cross, sib).wait_send()
            return carry

        lax.fori_loop(0, n, step, 0)

    for layer in range(lay):
        share_first(layer, 0)
    for layer in range(lay):
        def pass_on(offset, layer=layer):
            mode_copy(offset, layer).wait_recv()
            share_first(layer, offset)

        for_offsets(pass_on)
    for_offsets(lambda offset: aux_copy(offset).wait_recv())
    per_window = LANES // mode_local
    windows = [
        sum(arecv[index] for index in range(w * per_window, (w + 1) * per_window))
        for w in range(harm // LANES)
    ]

    share_second(0)
    for layer in range(lay):
        share_end(layer)
        if layer + 1 < lay:
            share_second(layer + 1)
        for piece in range(nb):
            cols = cut(piece)
            wide = mrecv[piece, layer].astype(jnp.float32).reshape(harm, rows)
            coeff = windows[piece]
            modes[:, cols] = wide.astype(jnp.bfloat16)
            scaled[0, :, cols] = (wide * coeff[lay + layer][None]).astype(jnp.bfloat16)
            scaled[1, :, cols] = (wide * coeff[layer][None]).astype(jnp.bfloat16)
        for kind in range(2):
            layer_s[layer, kind] = lax.dot_general(
                modes[...], scaled[kind], (((1,), (1,)), ((), ())),
                preferred_element_type=jnp.float32,
            ).astype(jnp.bfloat16)
        layer_s[layer, 2] = -layer_s[layer, 0]

    def piece_rows(quarter, half):
        size = rows // HALVES
        return pl.ds(pl.multiple_of(quarter * rows + half * size, size), size)

    def far_copy(level, distance, slot, part, half):
        return pltpu.make_async_remote_copy(
            src_ref=state.at[slot, part, piece_rows(blk, half)],
            dst_ref=land.at[level, part, piece_rows(blk, half)],
            send_sem=far_send.at[level, part, half],
            recv_sem=far_recv.at[level, part, half],
            device_id=(lax.rem(group + distance, n), blk),
            device_id_type=MESH,
        )

    def send_far(level, distance, slot, part):
        @pl.when(group + distance < n)
        def _():
            for half in range(HALVES):
                far_copy(level, distance, slot, part, half).start()

    def far_left(level):
        for part in range(4):
            for half in range(HALVES):
                far_copy(level, 1, 0, part, half).wait_send()

    def join_copy(slot, part, index, quarter, other):
        where = state.at[slot, part, pl.ds(pl.multiple_of(quarter * rows, rows), rows)]
        return pltpu.make_async_remote_copy(
            src_ref=where,
            dst_ref=where,
            send_sem=join_send.at[slot, part, index],
            recv_sem=join_recv.at[slot, part, index],
            device_id=(group, other),
            device_id_type=MESH,
        )

    def join_first(slot, part):
        join_copy(slot, part, 0, blk, cross).start()
        join_copy(slot, part, 1, blk, sib).start()

    def join_second(slot):
        for part in (1, 0):
            join_copy(slot, part, 0, cross, cross).wait_recv()
            join_copy(slot, part, 2, cross, sib).start()

    def join_end(slot):
        for part in (1, 0):
            join_copy(slot, part, 1, sib, sib).wait_recv()
            join_copy(slot, part, 2, sib_cross, sib).wait_recv()

    def relay_copy(level, part, half, index, piece, other):
        where = land.at[level, part, piece_rows(piece, half)]
        return pltpu.make_async_remote_copy(
            src_ref=where,
            dst_ref=where,
            send_sem=relay_send.at[level, part, half, index],
            recv_sem=relay_recv.at[level, part, half, index],
            device_id=(group, other),
            device_id_type=MESH,
        )

    def relay_first(level, part):
        for half in range(HALVES):
            far_copy(level, 1, 0, part, half).wait_recv()
            if part >= 2:
                relay_copy(level, part, half, 0, blk, cross).start()
                relay_copy(level, part, half, 1, blk, sib).start()

    def relay_second(level, part):
        for half in range(HALVES):
            relay_copy(level, part, half, 0, cross, cross).wait_recv()
            relay_copy(level, part, half, 2, cross, sib).start()

    def relay_end(level, part):
        for half in range(HALVES):
            relay_copy(level, part, half, 1, sib, sib).wait_recv()
            relay_copy(level, part, half, 2, sib_cross, sib).wait_recv()

    def chain(total, start, coupling, repeat):
        source = start if repeat == 0 else total
        total[...] = (start[...] + dot(source[...], coupling[...])).astype(jnp.bfloat16)

    def own_star(upper, lower, put, first, second, end, join):
        a11, a12, a21, a22 = upper
        b11, b12, b21, b22 = lower
        a11, a12, b21, b22 = [ref.at[own] for ref in (a11, a12, b21, b22)]
        first(3)
        join(0)
        second(3)
        join(1)
        end(3)
        up[...] = dot(a22[...], b11[...]).astype(jnp.bfloat16)
        for repeat in range(REFL):
            chain(right, b21, up, repeat)
        mid[...] = dot(right[...], a22[...]).astype(jnp.bfloat16)
        put(3, b22[...] + dot(mid[...], b12[...]))
        down[...] = dot(b11[...], a22[...]).astype(jnp.bfloat16)
        first(1)
        first(2)
        for repeat in range(REFL):
            chain(left, a12, down, repeat)
        put(1, dot(left[...], b12[...]))
        mid[...] = dot(left[...], b11[...]).astype(jnp.bfloat16)
        second(2)
        end(2)
        put(2, dot(right[...], a21[...]))
        first(0)
        put(0, a11[...] + dot(mid[...], a21[...]))

    def parts(ref):
        return [ref.at[part] for part in range(4)]

    def layer_parts(layer):
        refl, tran, back = [layer_s.at[layer, kind] for kind in range(3)]
        return [refl, tran, tran, back]

    def nothing(*where):
        pass

    last = levels - 1
    assert lay == 2 and nb == 4 and last >= 1
    def put_state(level, distance):
        def put(part, value):
            state[level, part, own] = value.astype(jnp.bfloat16)
            send_far(level, distance, level, part)
            if part < 2:
                join_first(level, part)

        return put

    own_star(
        layer_parts(0), layer_parts(1), put_state(0, 1), nothing, nothing, nothing, nothing
    )

    slot_end = sum(jnp.where(group >= (1 << k), 1, 0) for k in range(last))
    half = 1 << last

    def one_level(level, distance):
        @pl.when(group >= distance)
        def _():
            own_star(
                parts(land.at[level]), parts(state.at[level]), put_state(level + 1, 2 * distance),
                functools.partial(relay_first, level),
                functools.partial(relay_second, level),
                functools.partial(relay_end, level),
                lambda step: (join_second, join_end)[step](level),
            )

        @pl.when(group < distance)
        def _():
            @pl.when(jnp.logical_or(level == 0, 2 * group >= distance))
            def _():
                join_second(level)
                join_end(level)

            far_left(level)

            @pl.when(level == last - 2)
            def _():
                for part in (3, 1):
                    send_far(last, half, slot_end, part)

            for part in (3, 1):
                @pl.when(jnp.logical_or(level < last - 1, 4 * group >= half))
                def _(part=part):
                    send_far(level + 1, 2 * distance, slot_end, part)
            for part in (2, 0):
                send_far(level + 1, 2 * distance, slot_end, part)

        return 2 * distance

    lax.fori_loop(0, last, one_level, 1)

    @pl.when(group < half)
    def _():
        @pl.when(2 * group >= half)
        def _():
            join_second(last)
            join_end(last)

        out_ref[...] = state[slot_end, :, own]

    def put_out(part, value):
        out_ref[part] = value.astype(jnp.bfloat16)

    @pl.when(group >= half)
    def _():
        own_star(
            parts(land.at[last]), parts(state.at[last]), put_out,
            functools.partial(relay_first, last),
            functools.partial(relay_second, last),
            functools.partial(relay_end, last),
            lambda step: (join_second, join_end)[step](last),
        )

    for layer in range(lay):
        for_offsets(lambda offset: mode_copy(offset, layer).wait_send())
        share_left(layer)
    for_offsets(lambda offset: aux_copy(offset).wait_send())
    for level in range(levels):
        reach = 1 << level
        sends = group + reach < n
        if level < last:
            sends = jnp.logical_and(sends, group >= reach)

        @pl.when(sends)
        def _(level=level):
            far_left(level)

        @pl.when(group >= reach)
        def _(level=level):
            for part in (2, 3):
                for piece in range(HALVES):
                    relay_copy(level, part, piece, 0, blk, cross).wait_send()
                    relay_copy(level, part, piece, 1, blk, sib).wait_send()
                    relay_copy(level, part, piece, 2, cross, sib).wait_send()

        @pl.when(2 * group >= reach if level else group >= 0)
        def _(level=level):
            for part in range(2):
                join_copy(level, part, 0, blk, cross).wait_send()
                join_copy(level, part, 1, blk, sib).wait_send()
                join_copy(level, part, 2, cross, sib).wait_send()


def on_device(n, nb, mode_matrix, decay_rate, facet_refl):
    layers, mode_local = decay_rate.shape
    harm = n * mode_matrix.shape[1]
    lay = layers // n
    levels = n.bit_length() - 1
    refl = facet_refl.astype(jnp.float32)
    tran = jnp.sqrt(1.0 - refl * refl) * jnp.exp(-decay_rate.astype(jnp.float32))
    coeff = jnp.concatenate(
        [tran.reshape(n, lay, mode_local), refl.reshape(n, lay, mode_local)], axis=1
    )
    coeff = jnp.pad(coeff, ((0, 0), (0, 8 - 2 * lay), (0, 0)))
    copies = LANES // mode_local
    place = lax.broadcasted_iota(jnp.int32, (1, 1, LANES), 2) // mode_local
    aux = jnp.where(
        place == lax.rem(lax.axis_index("layer"), copies), jnp.tile(coeff, (1, 1, copies)), 0.0
    )
    square = (harm, harm)
    dma = pltpu.SemaphoreType.DMA
    vmem = pl.BlockSpec(memory_space=pltpu.VMEM)
    result = pl.pallas_call(
        functools.partial(stack_kernel, n, nb, levels),
        out_shape=jax.ShapeDtypeStruct((4, harm // nb, harm), jnp.bfloat16),
        in_specs=[vmem, vmem],
        out_specs=vmem,
        scratch_shapes=[
            pltpu.VMEM((nb, lay, n) + mode_matrix.shape[1:], jnp.bfloat16),
            pltpu.VMEM((n, 8, LANES), jnp.float32),
            pltpu.VMEM(square, jnp.bfloat16),
            pltpu.VMEM((2,) + square, jnp.bfloat16),
            pltpu.VMEM((lay, 3) + square, jnp.bfloat16),
            pltpu.VMEM((levels, 4) + square, jnp.bfloat16),
            pltpu.VMEM((levels, 4) + square, jnp.bfloat16),
        ]
        + [pltpu.VMEM(square, jnp.bfloat16)] * 2
        + [pltpu.VMEM((harm // nb, harm), jnp.bfloat16)] * 3
        + [dma((n, lay))] * 2
        + [dma((n,))] * 2
        + [dma((lay, n, 3))] * 2
        + [dma((levels, 4, HALVES))] * 2
        + [dma((levels, 4, HALVES, 3))] * 2
        + [dma((levels, 2, 3))] * 2,
        compiler_params=pltpu.CompilerParams(
            collective_id=0, has_side_effects=True, vmem_limit_bytes=56 * 1024 * 1024
        ),
        cost_estimate=pl.CostEstimate(
            flops=2 * harm**3 * 60, bytes_accessed=2**20, transcendentals=0
        ),
    )(mode_matrix, aux)
    return result[None]


def solution(mesh):
    n, nb = mesh.shape["layer"], mesh.shape["blk"]
    placed = (P(None, "layer", "blk"), P(None, "layer"), P(None, "layer"))
    return jax.shard_map(
        functools.partial(on_device, n, nb),
        mesh=mesh,
        in_specs=placed,
        out_specs=P("layer", None, "blk", None),
        check_vma=False,
    )
```
